512 devices in a mesh: tm: 64 (over z_hi, y, x), head: 8 (over z_lo, core).
Axes of the slice: x: 4, y: 8, z: 8 (z_hi: 2, z_lo: 4; z = z_hi * 4 + z_lo), core: 2. Of those that a mesh axis runs over, the one named last changes fastest.
Arguments:
- frames_in: bfloat16 [64, 1024, 1024], P('tm', 'head'), may hold values from -400 to 400
- in_weight: bfloat16 [1024, 5120], P('tm', 'head'), may hold values from -0.1875 to 0.1875
- out_weight: bfloat16 [1024, 1024], replicated, may hold values from -0.1875 to 0.1875
- block_ids: int32 [1024], replicated, may hold values from 0 to 15, as said below
- block_lists: int32 [16, 4], replicated, may hold values from 0 to 15, as said below
- decays: float32 [64, 16, 16], P('tm', 'head'), may hold values from 0.3 to 1
Outputs:
- layer_out: bfloat16 [64, 1024, 1024], P('tm', 'head')
The draws below stay inside these ranges and needn't reach their ends.
Inputs may be any that keep to these rules, and one draw needn't show every extreme that they name: `block_ids`: each of the 16 block ids is held by exactly 64 tokens. `block_lists`: row g starts with g itself, followed by 4 - 1 further blocks, all different.
All inputs are finite; a program needn't handle non-finite values.
Results may differ from the reference program's by a relative error of at most 0.0069.
Values may be sent and summed in bfloat16 or wider, within the bound.
A program may use at most 128 MiB of HBM per device.

```python
import math
import jax
import jax.numpy as jnp
from jax import lax

D = 1024
H = 16
HD = 64
N = 64
TOKS = 1024
NB = 16
K_SEL = 4
CLIP_IMAGE_COUNT = 64


def draw_frames_in(key, part):
    key_base, key_rows, key_cols = jax.random.split(key, 3)
    row_scale = jnp.exp(jax.random.uniform(key_rows, (CLIP_IMAGE_COUNT, TOKS, 1), jnp.float32) * math.log(10.0))
    col_scale = jnp.exp(jax.random.uniform(key_cols, (1, 1, D), jnp.float32) * math.log(10.0))
    base = jnp.clip(jax.random.normal(key_base, (CLIP_IMAGE_COUNT, TOKS, D), jnp.float32), -4.0, 4.0)
    return jnp.clip(base * row_scale * col_scale, -400.0, 400.0).astype(jnp.bfloat16)


def draw_block_ids(key, part):
    order = jax.random.permutation(jax.random.fold_in(key, 11), TOKS)
    return (order // (TOKS // NB)).astype(jnp.int32)


def draw_block_lists(key, part):
    base_key = jax.random.fold_in(key, 23)

    def one_row(index):
        others = jax.random.permutation(jax.random.fold_in(base_key, index), NB - 1)[:K_SEL - 1]
        chosen = (index + 1 + others) % NB
        return jnp.concatenate([jnp.full((1,), index, jnp.int32), chosen.astype(jnp.int32)])
    return jax.vmap(one_row)(jnp.arange(NB, dtype=jnp.int32)).astype(jnp.int32)


def draw_decays(key, part):
    variety_seed, gradual_seed, quick_seed, scatter_seed, spike_seed, strength_seed = jax.random.split(key, 6)
    share_fast = 0.5
    fast_head = jax.random.uniform(variety_seed, (1, H, 1), jnp.float32) < share_fast
    slow_rate = jnp.exp(jax.random.uniform(gradual_seed, (1, H, 1), jnp.float32, math.log(0.05), math.log(0.5))) / CLIP_IMAGE_COUNT
    fast_rate = jnp.exp(jax.random.uniform(quick_seed, (1, H, 1), jnp.float32, math.log(math.log(10.0) / 50.0), math.log(math.log(10.0) / 30.0)))
    resting_level = jnp.where(fast_head, fast_rate, slow_rate)
    level_variation = jnp.exp(jax.random.uniform(scatter_seed, (CLIP_IMAGE_COUNT, 1, NB), jnp.float32, math.log(0.5), math.log(2.0)))
    spike_beginning = jax.random.randint(spike_seed, (2,), 0, CLIP_IMAGE_COUNT)
    image_index_along_clip = jnp.arange(CLIP_IMAGE_COUNT, dtype=jnp.int32)[:, None, None]
    within_spike_window = (image_index_along_clip == spike_beginning[0]) | (image_index_along_clip == spike_beginning[1])
    fading_strength = jax.random.uniform(strength_seed, (CLIP_IMAGE_COUNT, H, NB), jnp.float32, 0.5, 0.8)
    kept_share = jnp.exp(-resting_level * level_variation) * jnp.where(within_spike_window, fading_strength, 1.0)
    return kept_share.astype(jnp.float32)


def steps_of(key, dims, cuts, low, high):
    level = 1.0
    for dim, blocks in cuts:
        steps = jax.random.uniform(jax.random.fold_in(jax.random.fold_in(key, 6), dim), (blocks,), jnp.float32, low / len(cuts), high / len(cuts))
        level = level * jnp.repeat(jnp.exp(steps), dims[dim] // blocks).reshape((-1,) + (1,) * (len(dims) - 1 - dim))
    return level


def scatter_about(stream_key, dims, scale, limit, pieces=(), kind=jnp.bfloat16):
    array = jax.random.normal(stream_key, dims, jnp.float32) * scale
    if len(pieces) > 0:
        array = steps_of(stream_key, dims, pieces, -0.22, 0.18) * array
    return jnp.clip(array, min=-limit, max=limit).astype(kind)


def setup_inputs(seed: int = 0) -> dict:
    streams_of = jax.random.split(jax.random.key(seed), 7)
    frames_in = draw_frames_in(jax.random.fold_in(streams_of[6], 71), 0)
    in_weight = scatter_about(streams_of[1], (D, 5 * H * HD), D ** -0.5, 0.1875, ((0, 64), (1, 8)))
    out_weight = scatter_about(streams_of[2], (H * HD, D), (H * HD) ** -0.5, 0.1875)
    block_ids = draw_block_ids(jax.random.fold_in(streams_of[6], 71), 0)
    block_lists = draw_block_lists(jax.random.fold_in(streams_of[6], 71), 0)
    decays = draw_decays(jax.random.fold_in(streams_of[6], 71), 0)
    return dict(frames_in=frames_in, in_weight=in_weight, out_weight=out_weight, block_ids=block_ids, block_lists=block_lists, decays=decays)


epsilon = 1e-06
highest = lax.Precision.HIGHEST

def head_norm(values):
    wide = values.astype(jnp.float32)
    return (wide * lax.rsqrt(lax.optimization_barrier(jnp.mean(wide * wide, axis=-1, keepdims=True)) + epsilon)).astype(jnp.bfloat16)

def reference(frames_in, in_weight, out_weight, block_ids, block_lists, decays):
    labels = jnp.arange(NB, dtype=jnp.int32)
    onehot = (block_ids[:, None] == labels[None, :]).astype(jnp.float32)
    adjacent = jnp.any(block_lists[:, :, None] == labels[None, None, :], axis=1).astype(jnp.float32)
    allowed = jnp.dot(jnp.dot(onehot, adjacent, precision=highest), onehot.T, precision=highest)
    ssm_scale = 1.0 / (N * math.sqrt(TOKS // NB))

    def frame_step(carry_state, inputs):
        frame_rows, frame_decay = inputs
        inputs_wide = frame_rows.astype(jnp.float32)
        normed = (inputs_wide * lax.rsqrt(lax.optimization_barrier(jnp.mean(inputs_wide * inputs_wide, axis=-1, keepdims=True)) + epsilon)).astype(jnp.bfloat16)
        projected = jnp.dot(normed, in_weight, preferred_element_type=jnp.float32).astype(jnp.bfloat16)
        projected = projected.reshape(TOKS, H, 5, HD)
        queries = head_norm(projected[:, :, 0]).astype(jnp.float32)
        key_rows = head_norm(projected[:, :, 1]).astype(jnp.float32)
        values = projected[:, :, 2].astype(jnp.float32)
        input_map = projected[:, :, 3, :N].astype(jnp.float32)
        output_map = projected[:, :, 4, :N].astype(jnp.float32)
        scores = jnp.einsum('shd,thd->hst', queries, key_rows, precision=highest) / math.sqrt(HD)
        exponent = jnp.exp(scores) * allowed[None]
        weights = (exponent / lax.optimization_barrier(jnp.sum(exponent, axis=-1, keepdims=True))).astype(jnp.bfloat16)
        attended = jnp.einsum('hst,thd->shd', weights.astype(jnp.float32), values, precision=highest)
        update = jnp.einsum('sb,shn,shd->hbnd', onehot, input_map, values, precision=highest)
        carry_state = frame_decay[:, :, None, None] * carry_state + update
        readout = jnp.einsum('sb,shn,hbnd->shd', onehot, output_map, carry_state, precision=highest) * ssm_scale
        mixed = (attended + readout).astype(jnp.bfloat16).reshape(TOKS, H * HD)
        result = jnp.dot(mixed, out_weight, preferred_element_type=jnp.float32).astype(jnp.bfloat16)
        return (carry_state, result)
    start_state = jnp.zeros((H, NB, N, HD), jnp.float32)
    final_state, frame_outs = lax.scan(frame_step, start_state, (frames_in, decays))
    return frame_outs
```

```python
import functools

import jax
import jax.numpy as jnp
from jax import lax
from jax.experimental import pallas as pl
from jax.experimental.pallas import tpu as pltpu
from jax.sharding import PartitionSpec as P

HD = 64
NB = 16
D = 1024
TOKS = 1024
LOCAL = 128
WIDE = 2 * HD
NX, NY, NZ = 4, 8, 2
NG = NY * NZ
LINE, CORES = 4, 2
HEADS_AXIS = LINE * CORES
CHUNKS = 2
ROWS = 256
EPS = 1e-6
FAR = -256.0
F32, BF16 = jnp.float32, jnp.bfloat16
MESH = pl.DeviceIdType.MESH


def kernel(
    x_ref, w_ref, wo_hbm, bid_ref, lists_ref, dec_ref, out_ref,
    xbuf, wbuf, wo, bidb, fmat, qa, ka, va, cc, acc, res,
    sslab, ubuf, sx, tslab, tbuf, cslab, cbuf, stslab, sbuf, sbd, mslab, mbuf,
    dout, dxbuf, pdout, pdbuf,
    wz_s, wz_r, wx_s, wx_r, wy_s, wy_r, xg_s, xg_r, sib_s, sib_r,
    dx_s, dx_r, pd_s, pd_r, u_s, u_r, t_s, t_r, c_s, c_r, st_s, st_r, m_s, m_r, wo_sem,
):
    tm, head = lax.axis_index("tm"), lax.axis_index("head")
    x, r = lax.rem(tm, NX), lax.div(tm, NX)
    y, zh = lax.rem(r, NY), lax.div(r, NY)
    z, core = lax.div(head, CORES), lax.rem(head, CORES)

    def send(src, dst, ssem, rsem, tm_to, head_to):
        copy = pltpu.make_async_remote_copy(
            src_ref=src, dst_ref=dst, send_sem=ssem, recv_sem=rsem,
            device_id=(tm_to, head_to), device_id_type=MESH,
        )
        copy.start()
        return copy

    def tm_of(group, xx):
        return group * NX + xx

    barrier = pltpu.get_barrier_semaphore()
    for k in range(1, HEADS_AXIS):
        pl.semaphore_signal(
            barrier, inc=1, device_id=(tm, lax.rem(head + k, HEADS_AXIS)), device_id_type=MESH
        )
    for k in range(1, NX):
        pl.semaphore_signal(
            barrier, inc=1, device_id=(tm_of(r, lax.rem(x + k, NX)), head), device_id_type=MESH
        )
    for k in range(1, NG):
        pl.semaphore_signal(
            barrier, inc=1, device_id=(tm_of(lax.rem(r + k, NG), x), head), device_id_type=MESH
        )

    lane = lax.broadcasted_iota(jnp.int32, (1, WIDE), 1)
    low = lane < HD
    wo_copy = pltpu.make_async_copy(wo_hbm, wo, wo_sem)
    wo_copy.start()

    raw = [w_ref[:, i * WIDE:(i + 1) * WIDE].astype(F32) for i in range(5)]
    swap = functools.partial(pltpu.roll, shift=HD, axis=1)
    ordered = [
        jnp.where(low, raw[0], raw[2]),
        swap(jnp.where(low, raw[3], raw[0])),
        jnp.where(low, raw[1], raw[3]),
        swap(jnp.where(low, raw[4], raw[1])),
        jnp.where(low, raw[2], raw[4]),
    ]
    mine = wbuf.at[zh, y, x]
    for i in range(5):
        mine[:, i * WIDE:(i + 1) * WIDE] = ordered[i].astype(BF16)
    pl.semaphore_wait(barrier, HEADS_AXIS - 1 + NX - 1 + NG - 1)
    wz = send(mine, mine, wz_s, wz_r, tm_of((1 - zh) * NY + y, x), head)

    wide = x_ref[0].astype(F32)
    xbuf[head] = (
        wide * lax.rsqrt(jnp.mean(wide * wide, axis=-1, keepdims=True) + EPS)
    ).astype(BF16)
    per = LOCAL // CHUNKS

    def part(source, k):
        return xbuf.at[source * CORES + core, pl.ds(k * per, per)]

    def line_copy(way, s, k, source):
        to = z + 1 if way == 0 else z - 1
        return pltpu.make_async_remote_copy(
            src_ref=part(source, k), dst_ref=part(source, k),
            send_sem=xg_s.at[way, s - 1, k], recv_sem=xg_r.at[way, s - 1, k],
            device_id=(tm, to * CORES + core), device_id_type=MESH,
        )

    def has_next(way):
        return z < LINE - 1 if way == 0 else z > 0

    def source_sent(way, s):
        return z - (s - 1) if way == 0 else z + (s - 1)

    def is_source(zz):
        return (zz >= 0) & (zz < LINE)

    def send_line(way, s, k):
        source = source_sent(way, s)

        @pl.when(has_next(way) & is_source(source))
        def _():
            line_copy(way, s, k, source).start()

    def sib_copy(source, k):
        return pltpu.make_async_remote_copy(
            src_ref=part(source, k), dst_ref=part(source, k),
            send_sem=sib_s.at[source, k], recv_sem=sib_r.at[source, k],
            device_id=(tm, z * CORES + 1 - core), device_id_type=MESH,
        )

    def take_line(s, k):
        for way in range(2):
            source = z - s if way == 0 else z + s

            @pl.when(is_source(source))
            def _(way=way, source=source):
                line_copy(way, s, k, source).wait_recv()
                if s < LINE - 1:
                    send_line(way, s + 1, k)
                sib_copy(source, k).start()

    for k in range(CHUNKS):
        for way in range(2):
            send_line(way, 1, k)
    for k in range(CHUNKS):
        sib_copy(z, k).start()

    dec = dec_ref[0]
    gi = lax.broadcasted_iota(jnp.int32, (NB, NB), 0)
    gj = lax.broadcasted_iota(jnp.int32, (NB, NB), 1)
    cols = [
        jnp.sum(jnp.where(gi == gj, dec[h:h + 1, :], 0.0), axis=1, keepdims=True) for h in range(2)
    ]
    drow = jnp.where(low, cols[0], cols[1])
    dout[...] = jnp.zeros_like(dout)
    for j in range(NX):
        dout[j, 0:4, :] = drow[4 * j:4 * j + 4, :]
    dxbuf[x] = dout[x]

    wz.wait_recv()
    pair = wbuf.at[:, y, x]
    wx, dx = [], []
    for k in range(1, NX):
        j = lax.rem(x + k, NX)
        wx.append(send(pair, pair, wx_s.at[k - 1], wx_r.at[k - 1], tm_of(r, j), head))
        dx.append(send(dout.at[j], dxbuf.at[x], dx_s.at[k - 1], dx_r.at[k - 1], tm_of(r, j), head))
    for c in wx:
        c.wait_recv()

    def ring(way, s):
        step = s - 1 if s else 0
        held = lax.rem(y - step + NY, NY) if way == 0 else lax.rem(y + step, NY)
        to = lax.rem(y + 1, NY) if way == 0 else lax.rem(y + NY - 1, NY)
        ref = wbuf.at[:, held] if s < NY // 2 else wbuf.at[pl.ds(way, 1), held]
        return send(ref, ref, wy_s.at[way, s - 1], wy_r.at[way, s - 1], tm_of(zh * NY + to, x), head)

    rings = [[ring(0, 1), ring(1, 1)]]
    take_line(1, 0)

    for c in dx:
        c.wait_recv()
    prod = dxbuf[0]
    for i in range(1, NX):
        prod = prod * dxbuf[i]
    pdout[...] = prod
    pdbuf[r] = prod
    pd = []
    for k in range(1, NG):
        j = lax.rem(r + k, NG)
        pd.append(send(pdout, pdbuf.at[r], pd_s.at[k - 1], pd_r.at[k - 1], tm_of(j, x), head))
    take_line(1, 1)

    ids = jnp.broadcast_to(bid_ref[...].astype(F32), (WIDE, TOKS))
    for i in range(TOKS // WIDE):
        rows = pl.ds(i * WIDE, WIDE)
        bidb[rows, :] = ids[:, i * WIDE:(i + 1) * WIDE].T
    fmat[...] = jnp.zeros_like(fmat)
    wrapped = lane & (HD - 1)
    adjacent = jnp.zeros((NB, WIDE), jnp.bool_)
    for k in range(lists_ref.shape[1]):
        adjacent = adjacent | (lists_ref[:, k:k + 1] == wrapped)
    fmat[0:NB, :] = jnp.where(adjacent | (wrapped >= NB), 0.0, FAR).astype(BF16)

    for c in rings[0]:
        c.wait_recv()
    rings.append([ring(0, 2), ring(1, 2)])
    take_line(2, 0)
    take_line(2, 1)
    for c in rings[1]:
        c.wait_recv()
    rings.append([ring(0, 3), ring(1, 3)])
    take_line(3, 0)
    for c in rings[2]:
        c.wait_recv()
    rings.append([ring(0, 4), ring(1, 4)])
    take_line(3, 1)
    for zz in range(LINE):
        for k in range(CHUNKS):
            sib_copy(zz, k).wait_recv()
    for c in rings[3]:
        c.wait_recv()

    acc[...] = jnp.zeros_like(acc)
    weights = wbuf[...].reshape(D, 5 * WIDE)
    wrapped_f = wrapped.astype(F32)

    def normed_heads(values):
        square = values * values
        means = [
            jnp.sum(jnp.where(keep, square, 0.0), axis=-1, keepdims=True) * (1.0 / HD)
            for keep in (low, ~low)
        ]
        return (values * lax.rsqrt(jnp.where(low, means[0], means[1]) + EPS)).astype(BF16).astype(F32)

    def project(i, _):
        rows = pl.ds(pl.multiple_of(i * ROWS, ROWS), ROWS)
        tokens = xbuf[pl.ds(i * (ROWS // LOCAL), ROWS // LOCAL)].reshape(ROWS, D)
        p = jnp.dot(tokens, weights, preferred_element_type=F32).astype(BF16)
        q, k, v, b, c = (p[:, j * WIDE:(j + 1) * WIDE] for j in range(5))
        ids = bidb[rows, :]
        hot = jnp.where(ids == wrapped_f, 1.0, 0.0)
        banned = jnp.dot(hot.astype(BF16), fmat[...], preferred_element_type=F32)
        qn = normed_heads(q.astype(F32)) * 0.125
        kn = normed_heads(k.astype(F32))
        v32 = v.astype(F32)
        qa[0, rows, :] = jnp.where(low, qn, banned).astype(BF16)
        qa[1, rows, :] = jnp.where(low, banned, qn).astype(BF16)
        ka[0, rows, :] = jnp.where(low, kn, hot).astype(BF16)
        ka[1, rows, :] = jnp.where(low, hot, kn).astype(BF16)
        va[0, rows, :] = jnp.where(low, v32, 1.0).astype(BF16)
        va[1, rows, :] = jnp.where(low, 1.0, v32).astype(BF16)
        cc[rows, :] = c
        bt = b.astype(F32).T.astype(BF16)
        for g in range(0, NB, 4):
            masked = jnp.concatenate(
                [jnp.where(ids == float(g + n), v32, 0.0).astype(BF16) for n in range(4)], axis=1
            )
            at = slice(g * WIDE, (g + 4) * WIDE)
            acc[:, at] += jnp.dot(bt, masked, preferred_element_type=F32)
        return 0

    lax.fori_loop(0, TOKS // ROWS, project, 0)

    for g in range(NB):
        at = slice(g * WIDE, (g + 1) * WIDE)
        both = jnp.where(low, acc[0:HD, at], acc[HD:WIDE, at])
        sslab[g // 4, (g % 4) * HD:(g % 4 + 1) * HD, :] = both.astype(BF16)
    up = []
    for k in range(1, NX):
        j = lax.rem(x + k, NX)
        up.append(send(sslab.at[j], ubuf.at[x], u_s.at[k - 1], u_r.at[k - 1], tm_of(r, j), head))
    ubuf[x] = sslab[x]

    def attend(first, last):
        def one(n, _):
            h, i = lax.div(n, TOKS // ROWS), lax.rem(n, TOKS // ROWS)
            rows = pl.ds(pl.multiple_of(i * ROWS, ROWS), ROWS)
            score = lax.dot_general(
                qa[h, rows, :], ka[h], (((1,), (1,)), ((), ())), preferred_element_type=F32
            )
            res[h, rows, :] = jnp.dot(
                jnp.exp(score).astype(BF16), va[h], preferred_element_type=F32
            )
            return 0

        lax.fori_loop(first, last, one, 0)

    attend(0, 3)
    for c in up:
        c.wait_recv()
    blocks = NB // NX
    for g in range(blocks):
        at = slice(g * HD, (g + 1) * HD)
        state = ubuf[0, at, :].astype(F32)
        sx[0, at, :] = state
        for i in range(1, NX):
            state = dxbuf[i, g:g + 1, :] * state + ubuf[i, at, :].astype(F32)
            sx[i, at, :] = state
        for n in range(HD // NB):
            tslab[g * (HD // NB) + n] = state[n * NB:(n + 1) * NB, :].astype(BF16)
    tot = []
    for k in range(1, NG):
        j = lax.rem(r + k, NG)
        tot.append(send(tslab.at[j], tbuf.at[r], t_s.at[k - 1], t_r.at[k - 1], tm_of(j, x), head))
    tbuf[r] = tslab[r]
    attend(3, 5)
    for c in pd:
        c.wait_recv()
    for c in tot:
        c.wait_recv()
    carry = jnp.zeros((NB, WIDE), F32)
    own_block = pl.ds(lax.div(r, HD // NB), 1)
    for i in range(NG):
        cslab[i] = carry.astype(BF16)
        carry = pdbuf[i, own_block, :] * carry + tbuf[i].astype(F32)
    back = []
    for k in range(1, NG):
        j = lax.rem(r + k, NG)
        back.append(send(cslab.at[j], cbuf.at[r], c_s.at[k - 1], c_r.at[k - 1], tm_of(j, x), head))
    cbuf[r] = cslab[r]
    attend(5, 7)
    for c in back:
        c.wait_recv()
    for g in range(blocks):
        at = slice(g * HD, (g + 1) * HD)
        came = cbuf[g * (HD // NB):(g + 1) * (HD // NB)].reshape(HD, WIDE).astype(F32)
        for i in range(NX):
            came = dxbuf[i, g:g + 1, :] * came
            stslab[i, at, :] = (sx[i, at, :] + came).astype(BF16)
    states = []
    for k in range(1, NX):
        j = lax.rem(x + k, NX)
        states.append(
            send(stslab.at[j], sbuf.at[x], st_s.at[k - 1], st_r.at[k - 1], tm_of(r, j), head)
        )
    sbuf[x] = stslab[x]
    attend(7, 8)
    for c in states:
        c.wait_recv()
    for g in range(NB):
        state = sbuf[g // blocks, (g % blocks) * HD:(g % blocks + 1) * HD, :].astype(F32)
        sbd[g * WIDE:g * WIDE + HD, :] = jnp.where(low, state, 0.0).astype(BF16)
        sbd[g * WIDE + HD:(g + 1) * WIDE, :] = jnp.where(low, 0.0, state).astype(BF16)

    def mix(i, _):
        rows = pl.ds(pl.multiple_of(i * ROWS, ROWS), ROWS)
        ids = bidb[rows, :]
        c32 = cc[rows, :].astype(F32)
        spread = jnp.concatenate(
            [jnp.where(ids == float(g), c32, 0.0).astype(BF16) for g in range(NB)], axis=1
        )
        readout = jnp.dot(spread, sbd[...], preferred_element_type=F32) * (1.0 / 512.0)
        first, second = res[0, rows, :], res[1, rows, :]
        total = pltpu.roll(jnp.where(low, second, first), HD, 1)
        mixed = (jnp.where(low, first, second) / total + readout).astype(BF16)
        mslab[pl.ds(i * (ROWS // LOCAL), ROWS // LOCAL)] = mixed.reshape(
            ROWS // LOCAL, LOCAL, WIDE
        )
        return 0

    lax.fori_loop(0, TOKS // ROWS, mix, 0)
    sent = []
    for k in range(1, HEADS_AXIS):
        j = lax.rem(head + k, HEADS_AXIS)
        sent.append(send(mslab.at[j], mbuf.at[head], m_s.at[k - 1], m_r.at[k - 1], tm, j))
    mbuf[head] = mslab[head]
    wo_copy.wait()
    for c in sent:
        c.wait_recv()
    full = jnp.concatenate([mbuf[i] for i in range(HEADS_AXIS)], axis=1)
    out_ref[0] = jnp.dot(full, wo[...], preferred_element_type=F32).astype(BF16)

    for c in (wz, *wx, *dx, *pd, *up, *tot, *back, *states, *sent, *(c for p in rings for c in p)):
        c.wait_send()
    for k in range(CHUNKS):
        for s in range(1, LINE):
            for way in range(2):
                source = source_sent(way, s)

                @pl.when(has_next(way) & is_source(source))
                def _(way=way, s=s, k=k, source=source):
                    line_copy(way, s, k, source).wait_send()
        for zz in range(LINE):
            sib_copy(zz, k).wait_send()


def body(frames_in, in_weight, out_weight, block_ids, block_lists, decays):
    vmem = pl.BlockSpec(memory_space=pltpu.VMEM)
    dma = pltpu.SemaphoreType.DMA
    scratch = [
        pltpu.VMEM((HEADS_AXIS, LOCAL, D), BF16),
        pltpu.VMEM((NZ, NY, NX, 16, 5 * WIDE), BF16),
        pltpu.VMEM((D, D), BF16),
        pltpu.VMEM((TOKS, WIDE), F32),
        pltpu.VMEM((WIDE, WIDE), BF16),
        pltpu.VMEM((2, TOKS, WIDE), BF16),
        pltpu.VMEM((2, TOKS, WIDE), BF16),
        pltpu.VMEM((2, TOKS, WIDE), BF16),
        pltpu.VMEM((TOKS, WIDE), BF16),
        pltpu.VMEM((WIDE, NB * WIDE), F32),
        pltpu.VMEM((2, TOKS, WIDE), F32),
        pltpu.VMEM((NX, 256, WIDE), BF16),
        pltpu.VMEM((NX, 256, WIDE), BF16),
        pltpu.VMEM((NX, 256, WIDE), F32),
        pltpu.VMEM((NG, NB, WIDE), BF16),
        pltpu.VMEM((NG, NB, WIDE), BF16),
        pltpu.VMEM((NG, NB, WIDE), BF16),
        pltpu.VMEM((NG, NB, WIDE), BF16),
        pltpu.VMEM((NX, 256, WIDE), BF16),
        pltpu.VMEM((NX, 256, WIDE), BF16),
        pltpu.VMEM((NB * WIDE, WIDE), BF16),
        pltpu.VMEM((HEADS_AXIS, LOCAL, WIDE), BF16),
        pltpu.VMEM((HEADS_AXIS, LOCAL, WIDE), BF16),
        pltpu.VMEM((NX, 8, WIDE), F32),
        pltpu.VMEM((NX, 8, WIDE), F32),
        pltpu.VMEM((8, WIDE), F32),
        pltpu.VMEM((NG, 8, WIDE), F32),
        dma, dma, dma((NX - 1,)), dma((NX - 1,)), dma((2, 4)), dma((2, 4)),
        dma((2, LINE - 1, CHUNKS)), dma((2, LINE - 1, CHUNKS)),
        dma((LINE, CHUNKS)), dma((LINE, CHUNKS)),
        dma((NX - 1,)), dma((NX - 1,)), dma((NG - 1,)), dma((NG - 1,)),
        dma((NX - 1,)), dma((NX - 1,)), dma((NG - 1,)), dma((NG - 1,)),
        dma((NG - 1,)), dma((NG - 1,)), dma((NX - 1,)), dma((NX - 1,)),
        dma((HEADS_AXIS - 1,)), dma((HEADS_AXIS - 1,)), dma,
    ]
    return pl.pallas_call(
        kernel,
        out_shape=jax.ShapeDtypeStruct((1, LOCAL, D), BF16),
        in_specs=[vmem, vmem, pl.BlockSpec(memory_space=pl.ANY), vmem, vmem, vmem],
        out_specs=vmem,
        scratch_shapes=scratch,
        compiler_params=pltpu.CompilerParams(
            collective_id=0, has_side_effects=True, vmem_limit_bytes=56 * 1024 * 1024
        ),
        name="layer",
    )(frames_in, in_weight, out_weight, block_ids.reshape(1, TOKS), block_lists, decays)


def solution(mesh):
    return jax.shard_map(
        body,
        mesh=mesh,
        in_specs=(P("tm", "head", None), P("tm", "head"), P(), P(), P(), P("tm", "head", None)),
        out_specs=P("tm", "head", None),
        check_vma=False,
    )
```

```python
import functools

import jax
import jax.numpy as jnp
from jax import lax
from jax.experimental import pallas as pl
from jax.experimental.pallas import tpu as pltpu
from jax.sharding import PartitionSpec as P

HD = 64
NB = 16
D = 1024
TOKS = 1024
LOCAL = 128
WIDE = 2 * HD
NX, NY, NZ = 4, 8, 2
NG = NY * NZ
LINE, CORES = 4, 2
HEADS_AXIS = LINE * CORES
CHUNKS = 2
ROWS = 256
EPS = 1e-6
FAR = -256.0
F32, BF16 = jnp.float32, jnp.bfloat16
MESH = pl.DeviceIdType.MESH


class Move:
    def __init__(self, copy, go=None, come=None):
        self.copy, self.go, self.come, self.took = copy, go, come, False

    def start(self):
        self.copy.start() if self.go is None else pl.when(self.go)(self.copy.start)

    def wait_recv(self):
        self.took = True
        self.copy.wait_recv() if self.come is None else pl.when(self.come)(self.copy.wait_recv)

    def wait_send(self):
        self.copy.wait_send() if self.go is None else pl.when(self.go)(self.copy.wait_send)


def kernel(
    x_hbm, w_hbm, wo_hbm, bid_ref, lists_ref, dec_ref, out_ref,
    xin, win, xbuf, wbuf, wo, bidb, fmat, qa, ka, va, cc, acc, res,
    sslab, ubuf, sx, tslab, tbuf, cslab, cbuf, stslab, sbuf, sbd, mslab, mbuf,
    dout, dxbuf, pdout, pdbuf,
    wz_s, wz_r, wx_s, wx_r, wy_s, wy_r, xg_s, xg_r, sib_s, sib_r,
    dx_s, dx_r, pd_s, pd_r, u_s, u_r, t_s, t_r, c_s, c_r, st_s, st_r, m_s, m_r, in_sem,
):
    tm, head = lax.axis_index("tm"), lax.axis_index("head")
    x, r = lax.rem(tm, NX), lax.div(tm, NX)
    y, zh = lax.rem(r, NY), lax.div(r, NY)
    z, core = lax.div(head, CORES), lax.rem(head, CORES)

    def tm_at(zz, yy, xx):
        return (zz * NY + yy) * NX + xx

    barrier = pltpu.get_barrier_semaphore()

    def greet(tm_to, head_to):
        pl.semaphore_signal(barrier, inc=1, device_id=(tm_to, head_to), device_id_type=MESH)

    greet(tm_at(1 - zh, y, x), head)
    greet(tm_at(zh, y, lax.rem(x + 2, NX)), head)
    for k in (1, NX - 1):
        greet(tm_at(zh, y, lax.rem(x + k, NX)), head)
    for k in (1, NY - 1):
        greet(tm_at(zh, lax.rem(y + k, NY), x), head)
    pl.when(z > 0)(lambda: greet(tm, head - CORES))
    pl.when(z < LINE - 1)(lambda: greet(tm, head + CORES))
    greet(tm, z * CORES + 1 - core)
    expected = 7 + (z > 0).astype(jnp.int32) + (z < LINE - 1).astype(jnp.int32)

    loads = [
        pltpu.make_async_copy(src, dst, in_sem.at[i])
        for i, (src, dst) in enumerate(((w_hbm, win), (x_hbm, xin), (wo_hbm, wo)))
    ]
    for load in loads:
        load.start()
    wo_copy = loads[2]
    started = []

    def send(src, dst, ssem, rsem, tm_to, head_to, go=None, come=None):
        move = Move(
            pltpu.make_async_remote_copy(
                src_ref=src, dst_ref=dst, send_sem=ssem, recv_sem=rsem,
                device_id=(tm_to, head_to), device_id_type=MESH,
            ), go, come,
        )
        move.start()
        started.append(move)
        return move

    lane = lax.broadcasted_iota(jnp.int32, (1, WIDE), 1)
    low = lane < HD

    dec = dec_ref[0]
    gi = lax.broadcasted_iota(jnp.int32, (NB, NB), 0)
    gj = lax.broadcasted_iota(jnp.int32, (NB, NB), 1)
    cols = [
        jnp.sum(jnp.where(gi == gj, dec[h:h + 1, :], 0.0), axis=1, keepdims=True) for h in range(2)
    ]
    drow = jnp.where(low, cols[0], cols[1])
    dout[...] = jnp.zeros_like(dout)
    for j in range(NX):
        dout[j, 0:4, :] = drow[4 * j:4 * j + 4, :]
    dxbuf[x] = dout[x]

    loads[0].wait()
    raw = [win[:, i * WIDE:(i + 1) * WIDE].astype(F32) for i in range(5)]
    swap = functools.partial(pltpu.roll, shift=HD, axis=1)
    ordered = [
        jnp.where(low, raw[1], raw[3]),
        swap(jnp.where(low, raw[4], raw[1])),
        jnp.where(low, raw[0], raw[2]),
        swap(jnp.where(low, raw[3], raw[0])),
        jnp.where(low, raw[2], raw[4]),
    ]
    mine = wbuf.at[zh, y, x]
    for i in range(5):
        mine[:, i * WIDE:(i + 1) * WIDE] = ordered[i].astype(BF16)

    loads[1].wait()
    wide = xin[0].astype(F32)
    xbuf[head] = (
        wide * lax.rsqrt(jnp.mean(wide * wide, axis=-1, keepdims=True) + EPS)
    ).astype(BF16)
    per = LOCAL // CHUNKS

    def part(source, k):
        return xbuf.at[source * CORES + core, pl.ds(k * per, per)]

    def is_source(zz):
        return (zz >= 0) & (zz < LINE)

    line, sib = {}, {}

    def send_line(way, s, k):
        source, to = (z - (s - 1), z + 1) if way == 0 else (z + (s - 1), z - 1)
        come = is_source(z - s if way == 0 else z + s)
        ref = part(source, k)
        line[way, s, k] = send(
            ref, ref, xg_s.at[way, s - 1, k], xg_r.at[way, s - 1, k], tm, to * CORES + core,
            is_source(source) & is_source(to), come,
        )

    def send_sib(n, source, k, go=None, come=None):
        ref = part(source, k)
        sib[n, k] = send(
            ref, ref, sib_s.at[n, k], sib_r.at[n, k], tm, z * CORES + 1 - core, go, come
        )

    def take_line(s, k):
        for way in range(2):
            move = line[way, s, k]
            move.wait_recv()
            if s < LINE - 1:
                send_line(way, s + 1, k)
            send_sib(2 * s - 1 + way, z - s if way == 0 else z + s, k, move.come, move.come)

    def send_x(side):
        ref = wbuf.at[zh if side == 0 else 1 - zh, y, x]
        return [
            send(ref, ref, wx_s.at[side, k - 1], wx_r.at[side, k - 1],
                 tm_at(zh, y, lax.rem(x + k, NX)), head)
            for k in range(1, NX)
        ]

    def send_ring(side, s):
        half = zh if side == 0 else 1 - zh
        moves = []
        for way in range(2) if s < NY // 2 else (side,):
            held = lax.rem(y - (s - 1) + NY, NY) if way == 0 else lax.rem(y + (s - 1), NY)
            to = lax.rem(y + (1 if way == 0 else NY - 1), NY)
            ref = wbuf.at[half, held]
            moves.append(
                send(ref, ref, wy_s.at[side, way, s - 1], wy_r.at[side, way, s - 1],
                     tm_at(zh, to, x), head)
            )
        return moves

    def take(moves):
        for move in moves:
            move.wait_recv()

    pl.semaphore_wait(barrier, expected)
    wz = send(mine, mine, wz_s.at[0], wz_r.at[0], tm_at(1 - zh, y, x), head)
    own = send_x(0)
    for k in range(CHUNKS):
        for way in range(2):
            send_line(way, 1, k)
        send_sib(0, z, k)
    dx = []
    for k in range(1, NX):
        j = lax.rem(x + k, NX)
        dx.append(
            send(dout.at[j], dxbuf.at[x], dx_s.at[k - 1], dx_r.at[k - 1], tm_at(zh, y, j), head)
        )
    take(own)
    rings = {(0, 1): send_ring(0, 1)}

    ids = jnp.broadcast_to(bid_ref[...].astype(F32), (WIDE, TOKS))
    for i in range(TOKS // WIDE):
        bidb[i * WIDE:(i + 1) * WIDE, :] = ids[:, i * WIDE:(i + 1) * WIDE].T
    fmat[...] = jnp.zeros_like(fmat)
    wrapped = lane & (HD - 1)
    wrapped_f = wrapped.astype(F32)
    key_block = lax.broadcasted_iota(jnp.int32, (WIDE, NB), 0) & (HD - 1)
    adjacent = key_block >= NB
    for k in range(lists_ref.shape[0]):
        adjacent = adjacent | (lists_ref[k:k + 1, :] == key_block)
    fmat[:, 0:NB] = jnp.where(adjacent, 0.0, FAR).astype(BF16)
    acc[...] = jnp.zeros_like(acc)

    def forward(side, s):
        take(rings[side, s])
        if s < NY // 2:
            rings[side, s + 1] = send_ring(side, s + 1)

    take_line(1, 0)
    wz.wait_recv()
    other = send_x(1)
    forward(0, 1)
    take_line(1, 1)
    take(other)
    rings[1, 1] = send_ring(1, 1)
    forward(0, 2)
    take_line(2, 0)
    forward(1, 1)
    forward(0, 3)
    take(dx)
    prod = dxbuf[0]
    for i in range(1, NX):
        prod = prod * dxbuf[i]
    pdout[...] = prod
    pdbuf[zh, y] = prod
    take_line(2, 1)
    forward(1, 2)
    take_line(3, 0)
    forward(0, 4)
    forward(1, 3)
    take_line(3, 1)
    for move in sib.values():
        move.wait_recv()
    forward(1, 4)

    first_half, second_half = zh == 0, zh == 1

    def to_group(src_of, dst, ssem, rsem):
        moves = []
        for k in range(NY):
            j = lax.rem(y + k, NY)
            moves.append(
                send(src_of(j), dst.at[0, y], ssem.at[1, k], rsem.at[1, k], tm_at(1, j, x), head,
                     first_half, second_half)
            )
        for k in range(1, NY):
            j = lax.rem(y + k, NY)
            moves.append(
                send(src_of(j), dst.at[zh, y], ssem.at[0, k], rsem.at[0, k], tm_at(zh, j, x), head)
            )
        return moves

    def project_vb(i, _):
        rows = pl.ds(pl.multiple_of(i * ROWS, ROWS), ROWS)
        tokens = xbuf[pl.ds(i * (ROWS // LOCAL), ROWS // LOCAL)].reshape(ROWS, D)
        weights = wbuf[:, :, :, :, 0:2 * WIDE].reshape(D, 2 * WIDE)
        p = jnp.dot(tokens, weights, preferred_element_type=F32).astype(BF16).astype(F32)
        v, b = p[:, 0:WIDE], p[:, WIDE:2 * WIDE]
        ids = bidb[rows, :]
        va[0, rows, :] = jnp.where(low, v, 1.0).astype(BF16)
        va[1, rows, :] = jnp.where(low, 1.0, v).astype(BF16)
        bt = b.T.astype(BF16)
        for g in range(0, NB, 4):
            masked = jnp.concatenate(
                [jnp.where(ids == float(g + n), v, 0.0).astype(BF16) for n in range(4)], axis=1
            )
            at = slice(g * WIDE, (g + 4) * WIDE)
            acc[:, at] += jnp.dot(bt, masked, preferred_element_type=F32)
        return 0

    lax.fori_loop(0, TOKS // ROWS, project_vb, 0)
    for g in range(NB):
        at = slice(g * WIDE, (g + 1) * WIDE)
        both = jnp.where(low, acc[0:HD, at], acc[HD:WIDE, at])
        sslab[g // 4, (g % 4) * HD:(g % 4 + 1) * HD, :] = both.astype(BF16)
    up = []
    for k in (2, 1, 3):
        j = lax.rem(x + k, NX)
        up.append(
            send(sslab.at[j], ubuf.at[x], u_s.at[k - 1], u_r.at[k - 1], tm_at(zh, y, j), head)
        )
    ubuf[x] = sslab[x]
    pd = to_group(lambda j: pdout, pdbuf, pd_s, pd_r)

    def normed_heads(values):
        square = values * values
        means = [
            jnp.sum(jnp.where(keep, square, 0.0), axis=-1, keepdims=True) * (1.0 / HD)
            for keep in (low, ~low)
        ]
        return (values * lax.rsqrt(jnp.where(low, means[0], means[1]) + EPS)).astype(BF16).astype(F32)

    def project_qkc(i, _):
        rows = pl.ds(pl.multiple_of(i * ROWS, ROWS), ROWS)
        tokens = xbuf[pl.ds(i * (ROWS // LOCAL), ROWS // LOCAL)].reshape(ROWS, D)
        weights = wbuf[:, :, :, :, 2 * WIDE:].reshape(D, 3 * WIDE)
        p = jnp.dot(tokens, weights, preferred_element_type=F32).astype(BF16)
        q, k, c = (p[:, j * WIDE:(j + 1) * WIDE] for j in range(3))
        hot = jnp.where(bidb[rows, :] == wrapped_f, 1.0, 0.0)
        banned = lax.dot_general(
            hot.astype(BF16), fmat[...], (((1,), (1,)), ((), ())), preferred_element_type=F32
        )
        qn = normed_heads(q.astype(F32)) * 0.125
        kn = normed_heads(k.astype(F32))
        qa[0, rows, :] = jnp.where(low, qn, banned).astype(BF16)
        qa[1, rows, :] = jnp.where(low, banned, qn).astype(BF16)
        ka[0, rows, :] = jnp.where(low, kn, hot).astype(BF16)
        ka[1, rows, :] = jnp.where(low, hot, kn).astype(BF16)
        cc[rows, :] = c
        return 0

    lax.fori_loop(0, TOKS // ROWS, project_qkc, 0)

    def attend(first, last):
        def one(n, _):
            h, i = lax.div(n, TOKS // ROWS), lax.rem(n, TOKS // ROWS)
            rows = pl.ds(pl.multiple_of(i * ROWS, ROWS), ROWS)
            score = lax.dot_general(
                qa[h, rows, :], ka[h], (((1,), (1,)), ((), ())), preferred_element_type=F32
            )
            res[h, rows, :] = jnp.dot(
                jnp.exp(score).astype(BF16), va[h], preferred_element_type=F32
            )
            return 0

        lax.fori_loop(first, last, one, 0)

    attend(0, 2)
    take(up)
    blocks, owned = NB // NX, 32
    for g in range(blocks):
        at = slice(g * HD, (g + 1) * HD)
        state = ubuf[0, at, :].astype(F32)
        sx[0, at, :] = state
        for i in range(1, NX):
            state = dxbuf[i, g:g + 1, :] * state + ubuf[i, at, :].astype(F32)
            sx[i, at, :] = state
        for n in range(HD // owned):
            piece = state[n * owned:(n + 1) * owned, :].astype(BF16)
            tslab[g * (HD // owned) + n] = piece
    tot = to_group(lambda j: tslab.at[j], tbuf, t_s, t_r)
    tbuf[zh, y] = tslab[y]
    attend(2, 6)
    take(pd)
    take(tot)
    own_block = pl.ds(lax.div(y, HD // owned), 1)
    before = jnp.zeros((owned, WIDE), F32)
    for i in range(NY):
        before = pdbuf[0, i, own_block, :] * before + tbuf[0, i].astype(F32)
    carry = before * zh.astype(F32)
    for i in range(NY):
        cslab[i] = carry.astype(BF16)
        carry = pdbuf[zh, i, own_block, :] * carry + tbuf[zh, i].astype(F32)
    back = []
    for k in range(1, NY):
        j = lax.rem(y + k, NY)
        back.append(
            send(cslab.at[j], cbuf.at[y], c_s.at[k - 1], c_r.at[k - 1], tm_at(zh, j, x), head)
        )
    cbuf[y] = cslab[y]
    attend(6, 8)
    take(back)
    for g in range(blocks):
        at = slice(g * HD, (g + 1) * HD)
        per_block = HD // owned
        came = cbuf[g * per_block:(g + 1) * per_block].reshape(HD, WIDE).astype(F32)
        for i in range(NX):
            came = dxbuf[i, g:g + 1, :] * came
            stslab[i, at, :] = (sx[i, at, :] + came).astype(BF16)
    states = []
    for k in (2, 1, 3):
        j = lax.rem(x + k, NX)
        states.append(
            send(stslab.at[j], sbuf.at[x], st_s.at[k - 1], st_r.at[k - 1], tm_at(zh, y, j), head)
        )
    sbuf[x] = stslab[x]

    def divide(i, _):
        rows = pl.ds(pl.multiple_of(i * ROWS, ROWS), ROWS)
        first, second = res[0, rows, :], res[1, rows, :]
        total = pltpu.roll(jnp.where(low, second, first), HD, 1)
        res[0, rows, :] = jnp.where(low, first, second) / total
        return 0

    lax.fori_loop(0, TOKS // ROWS, divide, 0)
    take(states)
    for g in range(NB):
        state = sbuf[g // blocks, (g % blocks) * HD:(g % blocks + 1) * HD, :].astype(F32)
        sbd[g * WIDE:g * WIDE + HD, :] = jnp.where(low, state, 0.0).astype(BF16)
        sbd[g * WIDE + HD:(g + 1) * WIDE, :] = jnp.where(low, 0.0, state).astype(BF16)
    sent = []
    odd = lax.rem(z, 2)
    for n, zz in enumerate((lax.rem(z + 2, LINE), 3 - z, z + 1 - 2 * odd, z)):
        rows = pl.ds(pl.multiple_of(zz * ROWS, ROWS), ROWS)
        ids = bidb[rows, :]
        c32 = cc[rows, :].astype(F32)
        spread = jnp.concatenate(
            [jnp.where(ids == float(g), c32, 0.0).astype(BF16) for g in range(NB)], axis=1
        )
        readout = jnp.dot(spread, sbd[...], preferred_element_type=F32) * (1.0 / 512.0)
        mixed = (res[0, rows, :] + readout).astype(BF16).reshape(CORES, LOCAL, WIDE)
        mslab[pl.ds(zz * CORES, CORES)] = mixed
        for to in (core, 1 - core):
            if n == LINE - 1 and to is core:
                continue
            dest = zz * CORES + to
            k = 2 * n + (0 if to is core else 1)
            sent.append(
                send(mslab.at[dest], mbuf.at[head], m_s.at[k], m_r.at[k], tm, dest)
            )
    mbuf[head] = mslab[head]
    wo_copy.wait()
    take(sent)
    full = jnp.concatenate([mbuf[i] for i in range(HEADS_AXIS)], axis=1)
    out_ref[0] = jnp.dot(full, wo[...], preferred_element_type=F32).astype(BF16)

    for move in started:
        move.wait_send()


def body(frames_in, in_weight, out_weight, block_ids, block_lists, decays):
    vmem = pl.BlockSpec(memory_space=pltpu.VMEM)
    dma = pltpu.SemaphoreType.DMA
    scratch = [
        pltpu.VMEM((1, LOCAL, D), BF16),
        pltpu.VMEM((16, 5 * WIDE), BF16),
        pltpu.VMEM((HEADS_AXIS, LOCAL, D), BF16),
        pltpu.VMEM((NZ, NY, NX, 16, 5 * WIDE), BF16),
        pltpu.VMEM((D, D), BF16),
        pltpu.VMEM((TOKS, WIDE), F32),
        pltpu.VMEM((WIDE, WIDE), BF16),
        pltpu.VMEM((2, TOKS, WIDE), BF16),
        pltpu.VMEM((2, TOKS, WIDE), BF16),
        pltpu.VMEM((2, TOKS, WIDE), BF16),
        pltpu.VMEM((TOKS, WIDE), BF16),
        pltpu.VMEM((WIDE, NB * WIDE), F32),
        pltpu.VMEM((2, TOKS, WIDE), F32),
        pltpu.VMEM((NX, 256, WIDE), BF16),
        pltpu.VMEM((NX, 256, WIDE), BF16),
        pltpu.VMEM((NX, 256, WIDE), F32),
        pltpu.VMEM((NY, 32, WIDE), BF16),
        pltpu.VMEM((NZ, NY, 32, WIDE), BF16),
        pltpu.VMEM((NY, 32, WIDE), BF16),
        pltpu.VMEM((NY, 32, WIDE), BF16),
        pltpu.VMEM((NX, 256, WIDE), BF16),
        pltpu.VMEM((NX, 256, WIDE), BF16),
        pltpu.VMEM((NB * WIDE, WIDE), BF16),
        pltpu.VMEM((HEADS_AXIS, LOCAL, WIDE), BF16),
        pltpu.VMEM((HEADS_AXIS, LOCAL, WIDE), BF16),
        pltpu.VMEM((NX, 8, WIDE), F32),
        pltpu.VMEM((NX, 8, WIDE), F32),
        pltpu.VMEM((8, WIDE), F32),
        pltpu.VMEM((NZ, NY, 8, WIDE), F32),
    ]
    for shape in (
        (1,), (2, NX - 1), (2, 2, NY // 2), (2, LINE - 1, CHUNKS), (2 * LINE - 1, CHUNKS),
        (NX - 1,), (2, NY), (NX - 1,), (2, NY), (NY - 1,), (NX - 1,), (HEADS_AXIS,),
    ):
        scratch += [dma(shape), dma(shape)]
    scratch.append(dma((3,)))
    hbm = pl.BlockSpec(memory_space=pl.ANY)
    return pl.pallas_call(
        kernel,
        out_shape=jax.ShapeDtypeStruct((1, LOCAL, D), BF16),
        in_specs=[hbm, hbm, hbm, vmem, vmem, vmem],
        out_specs=vmem,
        scratch_shapes=scratch,
        compiler_params=pltpu.CompilerParams(
            collective_id=0, has_side_effects=True, vmem_limit_bytes=56 * 1024 * 1024
        ),
        name="layer",
    )(frames_in, in_weight, out_weight, block_ids.reshape(1, TOKS), block_lists.T, decays)


def solution(mesh):
    return jax.shard_map(
        body,
        mesh=mesh,
        in_specs=(P("tm", "head", None), P("tm", "head"), P(), P(), P(), P("tm", "head", None)),
        out_specs=P("tm", "head", None),
        check_vma=False,
    )
```

```python
import functools

import jax
import jax.numpy as jnp
from jax import lax
from jax.experimental import pallas as pl
from jax.experimental.pallas import tpu as pltpu
from jax.sharding import PartitionSpec as P

HD = 64
NB = 16
D = 1024
TOKS = 1024
LOCAL = 128
WIDE = 2 * HD
NX, NY, NZ = 4, 8, 2
NG = NY * NZ
LINE, CORES = 4, 2
HEADS_AXIS = LINE * CORES
CHUNKS = 2
ROWS = 256
EPS = 1e-6
FAR = -256.0
F32, BF16 = jnp.float32, jnp.bfloat16
MESH = pl.DeviceIdType.MESH


class Move:
    def __init__(self, copy, go=None, come=None):
        self.copy, self.go, self.come, self.took = copy, go, come, False

    def start(self):
        self.copy.start() if self.go is None else pl.when(self.go)(self.copy.start)

    def wait_recv(self):
        self.took = True
        self.copy.wait_recv() if self.come is None else pl.when(self.come)(self.copy.wait_recv)

    def wait_send(self):
        self.copy.wait_send() if self.go is None else pl.when(self.go)(self.copy.wait_send)


def kernel(
    x_hbm, w_hbm, wo_hbm, bid_ref, lists_ref, dec_ref, out_ref,
    xin, win, xbuf, wvb, wqkc, wo, bidb, fmat, qa, ka, va, cc, acc, res,
    sslab, ubuf, sx, tslab, tbuf, cslab, cbuf, stslab, sbuf, sbd, mslab, mbuf,
    dout, dxbuf, pdout, pdbuf,
    wz_s, wz_r, wx_s, wx_r, wy_s, wy_r, xg_s, xg_r, sib_s, sib_r,
    dx_s, dx_r, pd_s, pd_r, u_s, u_r, t_s, t_r, c_s, c_r, st_s, st_r, m_s, m_r, in_sem,
):
    tm, head = lax.axis_index("tm"), lax.axis_index("head")
    x, r = lax.rem(tm, NX), lax.div(tm, NX)
    y, zh = lax.rem(r, NY), lax.div(r, NY)
    z, core = lax.div(head, CORES), lax.rem(head, CORES)

    def tm_at(zz, yy, xx):
        return (zz * NY + yy) * NX + xx

    barrier = pltpu.get_barrier_semaphore()

    def greet(tm_to, head_to):
        pl.semaphore_signal(barrier, inc=1, device_id=(tm_to, head_to), device_id_type=MESH)

    greet(tm_at(1 - zh, y, x), head)
    greet(tm_at(zh, y, lax.rem(x + 2, NX)), head)
    for k in (1, NX - 1):
        greet(tm_at(zh, y, lax.rem(x + k, NX)), head)
    for k in (1, NY - 1):
        greet(tm_at(zh, lax.rem(y + k, NY), x), head)
    pl.when(z > 0)(lambda: greet(tm, head - CORES))
    pl.when(z < LINE - 1)(lambda: greet(tm, head + CORES))
    greet(tm, z * CORES + 1 - core)
    expected = 7 + (z > 0).astype(jnp.int32) + (z < LINE - 1).astype(jnp.int32)

    loads = [
        pltpu.make_async_copy(src, dst, in_sem.at[i])
        for i, (src, dst) in enumerate(((w_hbm, win), (x_hbm, xin), (wo_hbm, wo)))
    ]
    for load in loads:
        load.start()
    wo_copy = loads[2]
    started = []

    def send(src, dst, ssem, rsem, tm_to, head_to, go=None, come=None):
        move = Move(
            pltpu.make_async_remote_copy(
                src_ref=src, dst_ref=dst, send_sem=ssem, recv_sem=rsem,
                device_id=(tm_to, head_to), device_id_type=MESH,
            ), go, come,
        )
        move.start()
        started.append(move)
        return move

    lane = lax.broadcasted_iota(jnp.int32, (1, WIDE), 1)
    low = lane < HD

    loads[0].wait()
    raw = [win[:, i * WIDE:(i + 1) * WIDE].astype(F32) for i in range(5)]
    swap = functools.partial(pltpu.roll, shift=HD, axis=1)
    ordered = [
        jnp.where(low, raw[1], raw[3]),
        swap(jnp.where(low, raw[4], raw[1])),
        jnp.where(low, raw[0], raw[2]),
        swap(jnp.where(low, raw[3], raw[0])),
        jnp.where(low, raw[2], raw[4]),
    ]
    for i in range(5):
        buf, col = (wvb, i) if i < 2 else (wqkc, i - 2)
        buf[zh, y, x, :, col * WIDE:(col + 1) * WIDE] = ordered[i].astype(BF16)

    per = LOCAL // CHUNKS

    def part(source, k):
        return xbuf.at[source * CORES + core, pl.ds(k * per, per)]

    def is_source(zz):
        return (zz >= 0) & (zz < LINE)

    line, sib = {}, {}

    def send_line(way, s, k):
        source, to = (z - (s - 1), z + 1) if way == 0 else (z + (s - 1), z - 1)
        come = is_source(z - s if way == 0 else z + s)
        ref = part(source, k)
        line[way, s, k] = send(
            ref, ref, xg_s.at[way, s - 1, k], xg_r.at[way, s - 1, k], tm, to * CORES + core,
            is_source(source) & is_source(to), come,
        )

    def send_sib(n, source, k, go=None, come=None):
        ref = part(source, k)
        sib[n, k] = send(
            ref, ref, sib_s.at[n, k], sib_r.at[n, k], tm, z * CORES + 1 - core, go, come
        )

    def take_line(s, k):
        for way in range(2):
            move = line[way, s, k]
            move.wait_recv()
            if s < LINE - 1:
                send_line(way, s + 1, k)
            send_sib(2 * s - 1 + way, z - s if way == 0 else z + s, k, move.come, move.come)

    parts = (wvb, wqkc)

    def send_z(c):
        ref = parts[c].at[zh, y, x]
        return [send(ref, ref, wz_s.at[c], wz_r.at[c], tm_at(1 - zh, y, x), head)]

    def send_x(c, side):
        ref = parts[c].at[zh if side == 0 else 1 - zh, y, x]
        return [
            send(ref, ref, wx_s.at[c, side, k - 1], wx_r.at[c, side, k - 1],
                 tm_at(zh, y, lax.rem(x + k, NX)), head)
            for k in range(1, NX)
        ]

    def take(moves):
        for move in moves:
            move.wait_recv()

    rings = {}

    def send_ring(c, side, s):
        half = zh if side == 0 else 1 - zh
        rings[c, side, s] = []
        for way in range(2) if s < NY // 2 else (side,):
            held = lax.rem(y - (s - 1) + NY, NY) if way == 0 else lax.rem(y + (s - 1), NY)
            to = lax.rem(y + (1 if way == 0 else NY - 1), NY)
            ref = parts[c].at[half, held]
            rings[c, side, s].append(
                send(ref, ref, wy_s.at[c, side, way, s - 1], wy_r.at[c, side, way, s - 1],
                     tm_at(zh, to, x), head)
            )

    def forward(c, side, s):
        take(rings[c, side, s])
        if s < NY // 2:
            send_ring(c, side, s + 1)

    pl.semaphore_wait(barrier, expected)
    far = send_z(0)
    own = send_x(0, 0)
    loads[1].wait()
    wide = xin[0].astype(F32)
    xbuf[head] = (
        wide * lax.rsqrt(jnp.mean(wide * wide, axis=-1, keepdims=True) + EPS)
    ).astype(BF16)
    for k in range(CHUNKS):
        for way in range(2):
            send_line(way, 1, k)
        send_sib(0, z, k)
    far_late = send_z(1)
    own_late = send_x(1, 0)
    take(own)
    send_ring(0, 0, 1)

    dec = dec_ref[0]
    gi = lax.broadcasted_iota(jnp.int32, (NB, NB), 0)
    gj = lax.broadcasted_iota(jnp.int32, (NB, NB), 1)
    cols = [
        jnp.sum(jnp.where(gi == gj, dec[h:h + 1, :], 0.0), axis=1, keepdims=True) for h in range(2)
    ]
    drow = jnp.where(low, cols[0], cols[1])
    dout[...] = jnp.zeros_like(dout)
    for j in range(NX):
        dout[j, 0:4, :] = drow[4 * j:4 * j + 4, :]
    dxbuf[x] = dout[x]

    dx = []
    for k in range(1, NX):
        j = lax.rem(x + k, NX)
        dx.append(
            send(dout.at[j], dxbuf.at[x], dx_s.at[k - 1], dx_r.at[k - 1], tm_at(zh, y, j), head)
        )
    take_line(1, 0)
    take(far)
    other = send_x(0, 1)
    forward(0, 0, 1)

    ids = jnp.broadcast_to(bid_ref[...].astype(F32), (WIDE, TOKS))
    for i in range(TOKS // WIDE):
        bidb[i * WIDE:(i + 1) * WIDE, :] = ids[:, i * WIDE:(i + 1) * WIDE].T
    fmat[...] = jnp.zeros_like(fmat)
    wrapped = lane & (HD - 1)
    wrapped_f = wrapped.astype(F32)
    key_block = lax.broadcasted_iota(jnp.int32, (WIDE, NB), 0) & (HD - 1)
    adjacent = key_block >= NB
    for k in range(lists_ref.shape[0]):
        adjacent = adjacent | (lists_ref[k:k + 1, :] == key_block)
    fmat[:, 0:NB] = jnp.where(adjacent, 0.0, FAR).astype(BF16)

    take_line(1, 1)
    take(other)
    send_ring(0, 1, 1)
    forward(0, 0, 2)
    take(far_late)
    other_late = send_x(1, 1)
    take_line(2, 0)
    forward(0, 1, 1)
    forward(0, 0, 3)
    take(own_late)
    send_ring(1, 0, 1)
    forward(0, 1, 2)
    take_line(2, 1)
    forward(0, 0, 4)
    forward(0, 1, 3)
    take(other_late)
    send_ring(1, 1, 1)
    take(dx)
    prod = dxbuf[0]
    for i in range(1, NX):
        prod = prod * dxbuf[i]
    pdout[...] = prod
    pdbuf[zh, y] = prod
    forward(1, 0, 1)
    forward(0, 1, 4)
    take_line(3, 0)

    def project_vb(zz, first):
        rows = pl.ds(pl.multiple_of(zz * ROWS, ROWS), ROWS)
        tokens = xbuf[pl.ds(zz * CORES, CORES)].reshape(ROWS, D)
        weights = wvb[...].reshape(D, 2 * WIDE)
        p = jnp.dot(tokens, weights, preferred_element_type=F32).astype(BF16).astype(F32)
        v, b = p[:, 0:WIDE], p[:, WIDE:2 * WIDE]
        ids = bidb[rows, :]
        va[0, rows, :] = jnp.where(low, v, 1.0).astype(BF16)
        va[1, rows, :] = jnp.where(low, 1.0, v).astype(BF16)
        bt = b.T.astype(BF16)
        for g in range(0, NB, 4):
            masked = jnp.concatenate(
                [jnp.where(ids == float(g + n), v, 0.0).astype(BF16) for n in range(4)], axis=1
            )
            at = slice(g * WIDE, (g + 4) * WIDE)
            term = jnp.dot(bt, masked, preferred_element_type=F32)
            acc[:, at] = term if first else acc[:, at] + term

    odd = lax.rem(z, 2)
    nearest = (z, z + 1 - 2 * odd, lax.rem(z + 2, LINE), 3 - z)
    for n in range(LINE):
        if n == LINE - 1:
            forward(1, 1, 1)
            take_line(3, 1)
        for way in range(2) if n else (0,):
            for k in range(CHUNKS):
                sib[2 * n - 1 + way if n else 0, k].wait_recv()
        project_vb(nearest[n], n == 0)

    first_half, second_half = zh == 0, zh == 1

    def to_group(src_of, dst, ssem, rsem):
        moves = []
        for k in range(NY):
            j = lax.rem(y + k, NY)
            moves.append(
                send(src_of(j), dst.at[0, y], ssem.at[1, k], rsem.at[1, k], tm_at(1, j, x), head,
                     first_half, second_half)
            )
        for k in range(1, NY):
            j = lax.rem(y + k, NY)
            moves.append(
                send(src_of(j), dst.at[zh, y], ssem.at[0, k], rsem.at[0, k], tm_at(zh, j, x), head)
            )
        return moves

    for g in range(NB):
        at = slice(g * WIDE, (g + 1) * WIDE)
        both = jnp.where(low, acc[0:HD, at], acc[HD:WIDE, at])
        sslab[g // 4, (g % 4) * HD:(g % 4 + 1) * HD, :] = both.astype(BF16)
    up = []
    for k in (2, 1, 3):
        j = lax.rem(x + k, NX)
        up.append(
            send(sslab.at[j], ubuf.at[x], u_s.at[k - 1], u_r.at[k - 1], tm_at(zh, y, j), head)
        )
    ubuf[x] = sslab[x]
    pd = to_group(lambda j: pdout, pdbuf, pd_s, pd_r)

    def normed_heads(values):
        square = values * values
        means = [
            jnp.sum(jnp.where(keep, square, 0.0), axis=-1, keepdims=True) * (1.0 / HD)
            for keep in (low, ~low)
        ]
        return (values * lax.rsqrt(jnp.where(low, means[0], means[1]) + EPS)).astype(BF16).astype(F32)

    def project_qkc(i, _):
        rows = pl.ds(pl.multiple_of(i * ROWS, ROWS), ROWS)
        tokens = xbuf[pl.ds(i * (ROWS // LOCAL), ROWS // LOCAL)].reshape(ROWS, D)
        weights = wqkc[...].reshape(D, 3 * WIDE)
        p = jnp.dot(tokens, weights, preferred_element_type=F32).astype(BF16)
        q, k, c = (p[:, j * WIDE:(j + 1) * WIDE] for j in range(3))
        hot = jnp.where(bidb[rows, :] == wrapped_f, 1.0, 0.0)
        banned = lax.dot_general(
            hot.astype(BF16), fmat[...], (((1,), (1,)), ((), ())), preferred_element_type=F32
        )
        qn = normed_heads(q.astype(F32)) * 0.125
        kn = normed_heads(k.astype(F32))
        qa[0, rows, :] = jnp.where(low, qn, banned).astype(BF16)
        qa[1, rows, :] = jnp.where(low, banned, qn).astype(BF16)
        ka[0, rows, :] = jnp.where(low, kn, hot).astype(BF16)
        ka[1, rows, :] = jnp.where(low, hot, kn).astype(BF16)
        cc[rows, :] = c
        return 0

    def attend(first, last):
        def one(n, _):
            h, i = lax.div(n, TOKS // ROWS), lax.rem(n, TOKS // ROWS)
            rows = pl.ds(pl.multiple_of(i * ROWS, ROWS), ROWS)
            score = lax.dot_general(
                qa[h, rows, :], ka[h], (((1,), (1,)), ((), ())), preferred_element_type=F32
            )
            res[h, rows, :] = jnp.dot(
                jnp.exp(score).astype(BF16), va[h], preferred_element_type=F32
            )
            return 0

        lax.fori_loop(first, last, one, 0)

    forward(1, 0, 2)
    forward(1, 1, 2)
    forward(1, 0, 3)
    take(up)
    blocks, owned = NB // NX, 32
    for g in range(blocks):
        at = slice(g * HD, (g + 1) * HD)
        state = ubuf[0, at, :].astype(F32)
        sx[0, at, :] = state
        for i in range(1, NX):
            state = dxbuf[i, g:g + 1, :] * state + ubuf[i, at, :].astype(F32)
            sx[i, at, :] = state
        for n in range(HD // owned):
            piece = state[n * owned:(n + 1) * owned, :].astype(BF16)
            tslab[g * (HD // owned) + n] = piece
    tot = to_group(lambda j: tslab.at[j], tbuf, t_s, t_r)
    tbuf[zh, y] = tslab[y]
    forward(1, 1, 3)
    take(rings[1, 0, NY // 2])
    take(rings[1, 1, NY // 2])
    lax.fori_loop(0, TOKS // ROWS, project_qkc, 0)
    attend(0, 3)
    take(pd)
    take(tot)
    own_block = pl.ds(lax.div(y, HD // owned), 1)
    before = jnp.zeros((owned, WIDE), F32)
    for i in range(NY):
        before = pdbuf[0, i, own_block, :] * before + tbuf[0, i].astype(F32)
    carry = before * zh.astype(F32)
    for i in range(NY):
        cslab[i] = carry.astype(BF16)
        carry = pdbuf[zh, i, own_block, :] * carry + tbuf[zh, i].astype(F32)
    back = []
    for k in range(1, NY):
        j = lax.rem(y + k, NY)
        back.append(
            send(cslab.at[j], cbuf.at[y], c_s.at[k - 1], c_r.at[k - 1], tm_at(zh, j, x), head)
        )
    cbuf[y] = cslab[y]
    attend(3, 8)
    take(back)
    for g in range(blocks):
        at = slice(g * HD, (g + 1) * HD)
        per_block = HD // owned
        came = cbuf[g * per_block:(g + 1) * per_block].reshape(HD, WIDE).astype(F32)
        for i in range(NX):
            came = dxbuf[i, g:g + 1, :] * came
            stslab[i, at, :] = (sx[i, at, :] + came).astype(BF16)
    states = []
    for k in (2, 1, 3):
        j = lax.rem(x + k, NX)
        states.append(
            send(stslab.at[j], sbuf.at[x], st_s.at[k - 1], st_r.at[k - 1], tm_at(zh, y, j), head)
        )
    sbuf[x] = stslab[x]

    def divide(i, _):
        rows = pl.ds(pl.multiple_of(i * ROWS, ROWS), ROWS)
        first, second = res[0, rows, :], res[1, rows, :]
        total = pltpu.roll(jnp.where(low, second, first), HD, 1)
        res[0, rows, :] = jnp.where(low, first, second) / total
        return 0

    lax.fori_loop(0, TOKS // ROWS, divide, 0)
    take(states)
    for g in range(NB):
        state = sbuf[g // blocks, (g % blocks) * HD:(g % blocks + 1) * HD, :].astype(F32)
        sbd[g * WIDE:g * WIDE + HD, :] = jnp.where(low, state, 0.0).astype(BF16)
        sbd[g * WIDE + HD:(g + 1) * WIDE, :] = jnp.where(low, 0.0, state).astype(BF16)
    sent = []
    for n, zz in enumerate((nearest[2], nearest[3], nearest[1], nearest[0])):
        rows = pl.ds(pl.multiple_of(zz * ROWS, ROWS), ROWS)
        ids = bidb[rows, :]
        c32 = cc[rows, :].astype(F32)
        spread = jnp.concatenate(
            [jnp.where(ids == float(g), c32, 0.0).astype(BF16) for g in range(NB)], axis=1
        )
        readout = jnp.dot(spread, sbd[...], preferred_element_type=F32) * (1.0 / 512.0)
        mixed = (res[0, rows, :] + readout).astype(BF16).reshape(CORES, LOCAL, WIDE)
        mslab[pl.ds(zz * CORES, CORES)] = mixed
        for to in (core, 1 - core):
            if n == LINE - 1 and to is core:
                continue
            dest = zz * CORES + to
            k = 2 * n + (0 if to is core else 1)
            sent.append(
                send(mslab.at[dest], mbuf.at[head], m_s.at[k], m_r.at[k], tm, dest)
            )
    mbuf[head] = mslab[head]
    wo_copy.wait()
    take(sent)
    full = jnp.concatenate([mbuf[i] for i in range(HEADS_AXIS)], axis=1)
    out_ref[0] = jnp.dot(full, wo[...], preferred_element_type=F32).astype(BF16)

    for move in started:
        move.wait_send()


def body(frames_in, in_weight, out_weight, block_ids, block_lists, decays):
    vmem = pl.BlockSpec(memory_space=pltpu.VMEM)
    dma = pltpu.SemaphoreType.DMA
    scratch = [
        pltpu.VMEM((1, LOCAL, D), BF16),
        pltpu.VMEM((16, 5 * WIDE), BF16),
        pltpu.VMEM((HEADS_AXIS, LOCAL, D), BF16),
        pltpu.VMEM((NZ, NY, NX, 16, 2 * WIDE), BF16),
        pltpu.VMEM((NZ, NY, NX, 16, 3 * WIDE), BF16),
        pltpu.VMEM((D, D), BF16),
        pltpu.VMEM((TOKS, WIDE), F32),
        pltpu.VMEM((WIDE, WIDE), BF16),
        pltpu.VMEM((2, TOKS, WIDE), BF16),
        pltpu.VMEM((2, TOKS, WIDE), BF16),
        pltpu.VMEM((2, TOKS, WIDE), BF16),
        pltpu.VMEM((TOKS, WIDE), BF16),
        pltpu.VMEM((WIDE, NB * WIDE), F32),
        pltpu.VMEM((2, TOKS, WIDE), F32),
        pltpu.VMEM((NX, 256, WIDE), BF16),
        pltpu.VMEM((NX, 256, WIDE), BF16),
        pltpu.VMEM((NX, 256, WIDE), F32),
        pltpu.VMEM((NY, 32, WIDE), BF16),
        pltpu.VMEM((NZ, NY, 32, WIDE), BF16),
        pltpu.VMEM((NY, 32, WIDE), BF16),
        pltpu.VMEM((NY, 32, WIDE), BF16),
        pltpu.VMEM((NX, 256, WIDE), BF16),
        pltpu.VMEM((NX, 256, WIDE), BF16),
        pltpu.VMEM((NB * WIDE, WIDE), BF16),
        pltpu.VMEM((HEADS_AXIS, LOCAL, WIDE), BF16),
        pltpu.VMEM((HEADS_AXIS, LOCAL, WIDE), BF16),
        pltpu.VMEM((NX, 8, WIDE), F32),
        pltpu.VMEM((NX, 8, WIDE), F32),
        pltpu.VMEM((8, WIDE), F32),
        pltpu.VMEM((NZ, NY, 8, WIDE), F32),
    ]
    for shape in (
        (2,), (2, 2, NX - 1), (2, 2, 2, NY // 2), (2, LINE - 1, CHUNKS), (2 * LINE - 1, CHUNKS),
        (NX - 1,), (2, NY), (NX - 1,), (2, NY), (NY - 1,), (NX - 1,), (HEADS_AXIS,),
    ):
        scratch += [dma(shape), dma(shape)]
    scratch.append(dma((3,)))
    hbm = pl.BlockSpec(memory_space=pl.ANY)
    return pl.pallas_call(
        kernel,
        out_shape=jax.ShapeDtypeStruct((1, LOCAL, D), BF16),
        in_specs=[hbm, hbm, hbm, vmem, vmem, vmem],
        out_specs=vmem,
        scratch_shapes=scratch,
        compiler_params=pltpu.CompilerParams(
            collective_id=0, has_side_effects=True, vmem_limit_bytes=56 * 1024 * 1024
        ),
        name="layer",
    )(frames_in, in_weight, out_weight, block_ids.reshape(1, TOKS), block_lists.T, decays)


def solution(mesh):
    return jax.shard_map(
        body,
        mesh=mesh,
        in_specs=(P("tm", "head", None), P("tm", "head"), P(), P(), P(), P("tm", "head", None)),
        out_specs=P("tm", "head", None),
        check_vma=False,
    )
```

```python
import functools

import jax
import jax.numpy as jnp
from jax import lax
from jax.experimental import pallas as pl
from jax.experimental.pallas import tpu as pltpu
from jax.sharding import PartitionSpec as P

HD = 64
NB = 16
D = 1024
TOKS = 1024
LOCAL = 128
WIDE = 2 * HD
NX, NY, NZ = 4, 8, 2
NG = NY * NZ
LINE, CORES = 4, 2
HEADS_AXIS = LINE * CORES
CHUNKS = 4
PAIRS = 2
ROWS = 256
EPS = 1e-6
FAR = -256.0
F32, BF16 = jnp.float32, jnp.bfloat16
MESH = pl.DeviceIdType.MESH


class Move:
    def __init__(self, copy, go=None, come=None):
        self.copy, self.go, self.come, self.took = copy, go, come, False

    def start(self):
        self.copy.start() if self.go is None else pl.when(self.go)(self.copy.start)

    def wait_recv(self):
        self.took = True
        self.copy.wait_recv() if self.come is None else pl.when(self.come)(self.copy.wait_recv)

    def wait_send(self):
        self.copy.wait_send() if self.go is None else pl.when(self.go)(self.copy.wait_send)


def kernel(
    x_hbm, w_hbm, wo_hbm, bid_ref, lists_ref, dec_ref, out_ref,
    xin, win, xbuf, wvb, wqkc, wo, bidb, fmat, qa, ka, va, cc, acc, res,
    sslab, ubuf, sx, tslab, tbuf, cslab, cbuf, stslab, sbuf, sbd, mslab, mbuf,
    dout, dxbuf, pdout, pdbuf,
    wz_s, wz_r, wx_s, wx_r, wd_s, wd_r, wy_s, wy_r, xg_s, xg_r, sib_s, sib_r,
    dx_s, dx_r, pd_s, pd_r, u_s, u_r, t_s, t_r, c_s, c_r, st_s, st_r, m_s, m_r, in_sem,
):
    tm, head = lax.axis_index("tm"), lax.axis_index("head")
    x, r = lax.rem(tm, NX), lax.div(tm, NX)
    y, zh = lax.rem(r, NY), lax.div(r, NY)
    z, core = lax.div(head, CORES), lax.rem(head, CORES)

    def tm_at(zz, yy, xx):
        return (zz * NY + yy) * NX + xx

    barrier = pltpu.get_barrier_semaphore()

    def greet(tm_to, head_to):
        pl.semaphore_signal(barrier, inc=1, device_id=(tm_to, head_to), device_id_type=MESH)

    greet(tm_at(1 - zh, y, x), head)
    greet(tm_at(zh, y, lax.rem(x + 2, NX)), head)
    for k in (1, NX - 1):
        greet(tm_at(zh, y, lax.rem(x + k, NX)), head)
    for k in (4, 3, 5, 2, 6, 1, 7):
        greet(tm_at(zh, lax.rem(y + k, NY), x), head)
    pl.when(z > 0)(lambda: greet(tm, head - CORES))
    pl.when(z < LINE - 1)(lambda: greet(tm, head + CORES))
    greet(tm, z * CORES + 1 - core)
    expected = 12 + (z > 0).astype(jnp.int32) + (z < LINE - 1).astype(jnp.int32)

    loads = [
        pltpu.make_async_copy(src, dst, in_sem.at[i])
        for i, (src, dst) in enumerate(((w_hbm, win), (x_hbm, xin), (wo_hbm, wo)))
    ]
    for load in loads:
        load.start()
    wo_copy = loads[2]
    started = []

    def send(src, dst, ssem, rsem, tm_to, head_to, go=None, come=None):
        move = Move(
            pltpu.make_async_remote_copy(
                src_ref=src, dst_ref=dst, send_sem=ssem, recv_sem=rsem,
                device_id=(tm_to, head_to), device_id_type=MESH,
            ), go, come,
        )
        move.start()
        started.append(move)
        return move

    lane = lax.broadcasted_iota(jnp.int32, (1, WIDE), 1)
    low = lane < HD

    loads[0].wait()
    raw = [win[:, i * WIDE:(i + 1) * WIDE].astype(F32) for i in range(5)]
    swap = functools.partial(pltpu.roll, shift=HD, axis=1)
    ordered = [
        jnp.where(low, raw[1], raw[3]),
        swap(jnp.where(low, raw[4], raw[1])),
        jnp.where(low, raw[0], raw[2]),
        swap(jnp.where(low, raw[3], raw[0])),
        jnp.where(low, raw[2], raw[4]),
    ]
    for i in range(5):
        buf, col = (wvb, i) if i < 2 else (wqkc, i - 2)
        buf[zh, y, x, :, col * WIDE:(col + 1) * WIDE] = ordered[i].astype(BF16)


    def part(source, k, size=LOCAL // CHUNKS):
        return xbuf.at[source * CORES + core, pl.ds(k * size, size)]

    def is_source(zz):
        return (zz >= 0) & (zz < LINE)

    line, sib = {}, {}

    def send_line(way, s, k):
        source, to = (z - (s - 1), z + 1) if way == 0 else (z + (s - 1), z - 1)
        come = is_source(z - s if way == 0 else z + s)
        ref = part(source, k)
        line[way, s, k] = send(
            ref, ref, xg_s.at[way, s - 1, k], xg_r.at[way, s - 1, k], tm, to * CORES + core,
            is_source(source) & is_source(to), come,
        )

    def send_sib(n, source, k, go=None, come=None):
        ref = part(source, k, LOCAL // PAIRS)
        sib[n, k] = send(
            ref, ref, sib_s.at[n, k], sib_r.at[n, k], tm, z * CORES + 1 - core, go, come
        )

    def take_line(s, k):
        for way in range(2):
            move = line[way, s, k]
            move.wait_recv()
            if s < LINE - 1:
                send_line(way, s + 1, k)
            if k % (CHUNKS // PAIRS) == CHUNKS // PAIRS - 1:
                send_sib(
                    2 * s - 1 + way, z - s if way == 0 else z + s, k // (CHUNKS // PAIRS),
                    move.come, move.come,
                )

    parts = (wvb, wqkc)

    def send_z(c):
        ref = parts[c].at[zh, y, x]
        return [send(ref, ref, wz_s.at[c], wz_r.at[c], tm_at(1 - zh, y, x), head)]

    def send_x(c, side):
        ref = parts[c].at[zh if side == 0 else 1 - zh, y, x]
        return [
            send(ref, ref, wx_s.at[c, side, k - 1], wx_r.at[c, side, k - 1],
                 tm_at(zh, y, lax.rem(x + k, NX)), head)
            for k in range(1, NX)
        ]

    def take(moves):
        for move in moves:
            move.wait_recv()

    rings = {}

    def send_y(side):
        ref = wvb.at[zh if side == 0 else 1 - zh, y]
        return [
            send(ref, ref, wd_s.at[side, k - 1], wd_r.at[side, k - 1],
                 tm_at(zh, lax.rem(y + k, NY), x), head)
            for k in (4, 3, 5, 2, 6, 1, 7)
        ]

    def send_ring(side, s):
        half = zh if side == 0 else 1 - zh
        rings[side, s] = []
        for way in range(2) if s < NY // 2 else (side,):
            held = lax.rem(y - (s - 1) + NY, NY) if way == 0 else lax.rem(y + (s - 1), NY)
            to = lax.rem(y + (1 if way == 0 else NY - 1), NY)
            ref = wqkc.at[half, held]
            rings[side, s].append(
                send(ref, ref, wy_s.at[side, way, s - 1], wy_r.at[side, way, s - 1],
                     tm_at(zh, to, x), head)
            )

    def forward(side, s):
        take(rings[side, s])
        if s < NY // 2:
            send_ring(side, s + 1)

    pl.semaphore_wait(barrier, expected)
    far = send_z(0)
    own = send_x(0, 0)
    loads[1].wait()
    wide = xin[0].astype(F32)
    xbuf[head] = (
        wide * lax.rsqrt(jnp.mean(wide * wide, axis=-1, keepdims=True) + EPS)
    ).astype(BF16)
    for k in range(CHUNKS):
        for way in range(2):
            send_line(way, 1, k)
    for k in range(PAIRS):
        send_sib(0, z, k)
    far_late = send_z(1)
    own_late = send_x(1, 0)
    take(own)
    direct = send_y(0)

    dec = dec_ref[0]
    gi = lax.broadcasted_iota(jnp.int32, (NB, NB), 0)
    gj = lax.broadcasted_iota(jnp.int32, (NB, NB), 1)
    cols = [
        jnp.sum(jnp.where(gi == gj, dec[h:h + 1, :], 0.0), axis=1, keepdims=True) for h in range(2)
    ]
    drow = jnp.where(low, cols[0], cols[1])
    dout[...] = jnp.zeros_like(dout)
    for j in range(NX):
        dout[j, 0:4, :] = drow[4 * j:4 * j + 4, :]
    dxbuf[x] = dout[x]

    dx = []
    for k in range(1, NX):
        j = lax.rem(x + k, NX)
        dx.append(
            send(dout.at[j], dxbuf.at[x], dx_s.at[k - 1], dx_r.at[k - 1], tm_at(zh, y, j), head)
        )
    take_line(1, 0)
    take(far)
    other = send_x(0, 1)
    take_line(1, 1)

    ids = jnp.broadcast_to(bid_ref[...].astype(F32), (WIDE, TOKS))
    for i in range(TOKS // WIDE):
        bidb[i * WIDE:(i + 1) * WIDE, :] = ids[:, i * WIDE:(i + 1) * WIDE].T
    fmat[...] = jnp.zeros_like(fmat)
    wrapped = lane & (HD - 1)
    wrapped_f = wrapped.astype(F32)
    key_block = lax.broadcasted_iota(jnp.int32, (WIDE, NB), 0) & (HD - 1)
    adjacent = key_block >= NB
    for k in range(lists_ref.shape[0]):
        adjacent = adjacent | (lists_ref[k:k + 1, :] == key_block)
    fmat[:, 0:NB] = jnp.where(adjacent, 0.0, FAR).astype(BF16)

    take_line(1, 2)
    take(other)
    direct += send_y(1)
    take_line(1, 3)
    take(far_late)
    other_late = send_x(1, 1)
    take_line(2, 0)
    take_line(2, 1)
    take(own_late)
    send_ring(0, 1)
    take_line(2, 2)
    take(dx)
    prod = dxbuf[0]
    for i in range(1, NX):
        prod = prod * dxbuf[i]
    pdout[...] = prod
    pdbuf[zh, y] = prod
    take_line(2, 3)
    take(other_late)
    send_ring(1, 1)
    take_line(3, 0)
    take_line(3, 1)
    take(direct)

    def project_vb(zz, first):
        rows = pl.ds(pl.multiple_of(zz * ROWS, ROWS), ROWS)
        tokens = xbuf[pl.ds(zz * CORES, CORES)].reshape(ROWS, D)
        weights = wvb[...].reshape(D, 2 * WIDE)
        p = jnp.dot(tokens, weights, preferred_element_type=F32).astype(BF16).astype(F32)
        v, b = p[:, 0:WIDE], p[:, WIDE:2 * WIDE]
        ids = bidb[rows, :]
        va[0, rows, :] = jnp.where(low, v, 1.0).astype(BF16)
        va[1, rows, :] = jnp.where(low, 1.0, v).astype(BF16)
        bt = b.T.astype(BF16)
        for g in range(0, NB, 4):
            masked = jnp.concatenate(
                [jnp.where(ids == float(g + n), v, 0.0).astype(BF16) for n in range(4)], axis=1
            )
            at = slice(g * WIDE, (g + 4) * WIDE)
            term = jnp.dot(bt, masked, preferred_element_type=F32)
            acc[:, at] = term if first else acc[:, at] + term

    odd = lax.rem(z, 2)
    nearest = (z, z + 1 - 2 * odd, lax.rem(z + 2, LINE), 3 - z)
    for n in range(LINE):
        if n == LINE - 1:
            take_line(3, 2)
            take_line(3, 3)
        for way in range(2) if n else (0,):
            for k in range(PAIRS):
                sib[2 * n - 1 + way if n else 0, k].wait_recv()
        project_vb(nearest[n], n == 0)

    first_half, second_half = zh == 0, zh == 1

    def to_group(src_of, dst, ssem, rsem):
        moves = []
        for k in range(NY):
            j = lax.rem(y + k, NY)
            moves.append(
                send(src_of(j), dst.at[0, y], ssem.at[1, k], rsem.at[1, k], tm_at(1, j, x), head,
                     first_half, second_half)
            )
        for k in range(1, NY):
            j = lax.rem(y + k, NY)
            moves.append(
                send(src_of(j), dst.at[zh, y], ssem.at[0, k], rsem.at[0, k], tm_at(zh, j, x), head)
            )
        return moves

    for g in range(NB):
        at = slice(g * WIDE, (g + 1) * WIDE)
        both = jnp.where(low, acc[0:HD, at], acc[HD:WIDE, at])
        sslab[g // 4, (g % 4) * HD:(g % 4 + 1) * HD, :] = both.astype(BF16)
    up = []
    for k in (2, 1, 3):
        j = lax.rem(x + k, NX)
        up.append(
            send(sslab.at[j], ubuf.at[x], u_s.at[k - 1], u_r.at[k - 1], tm_at(zh, y, j), head)
        )
    ubuf[x] = sslab[x]
    forward(0, 1)
    forward(1, 1)
    pd = to_group(lambda j: pdout, pdbuf, pd_s, pd_r)

    def normed_heads(values):
        square = values * values
        means = [
            jnp.sum(jnp.where(keep, square, 0.0), axis=-1, keepdims=True) * (1.0 / HD)
            for keep in (low, ~low)
        ]
        return (values * lax.rsqrt(jnp.where(low, means[0], means[1]) + EPS)).astype(BF16).astype(F32)

    def project_qkc():
        tokens = xbuf[...].reshape(TOKS, D)
        weights = wqkc[...].reshape(D, 3 * WIDE)
        p = jnp.dot(tokens, weights, preferred_element_type=F32).astype(BF16)
        q, k, c = (p[:, j * WIDE:(j + 1) * WIDE] for j in range(3))
        hot = jnp.where(bidb[...] == wrapped_f, 1.0, 0.0)
        banned = lax.dot_general(
            hot.astype(BF16), fmat[...], (((1,), (1,)), ((), ())), preferred_element_type=F32
        )
        qn = normed_heads(q.astype(F32)) * 0.125
        kn = normed_heads(k.astype(F32))
        qa[0, :, :] = jnp.where(low, qn, banned).astype(BF16)
        qa[1, :, :] = jnp.where(low, banned, qn).astype(BF16)
        ka[0, :, :] = jnp.where(low, kn, hot).astype(BF16)
        ka[1, :, :] = jnp.where(low, hot, kn).astype(BF16)
        cc[...] = c

    def attend(h):
        score = lax.dot_general(
            qa[h], ka[h], (((1,), (1,)), ((), ())), preferred_element_type=F32
        )
        res[h] = jnp.dot(jnp.exp(score).astype(BF16), va[h], preferred_element_type=F32)

    forward(0, 2)
    forward(1, 2)
    take(up)
    blocks, owned = NB // NX, 32
    for g in range(blocks):
        at = slice(g * HD, (g + 1) * HD)
        state = ubuf[0, at, :].astype(F32)
        sx[0, at, :] = state
        for i in range(1, NX):
            state = dxbuf[i, g:g + 1, :] * state + ubuf[i, at, :].astype(F32)
            sx[i, at, :] = state
        for n in range(HD // owned):
            piece = state[n * owned:(n + 1) * owned, :].astype(BF16)
            tslab[g * (HD // owned) + n] = piece
    tot = to_group(lambda j: tslab.at[j], tbuf, t_s, t_r)
    tbuf[zh, y] = tslab[y]
    forward(0, 3)
    forward(1, 3)
    take(rings[0, NY // 2])
    take(rings[1, NY // 2])
    project_qkc()
    attend(0)
    take(pd)
    take(tot)
    own_block = pl.ds(lax.div(y, HD // owned), 1)
    before = jnp.zeros((owned, WIDE), F32)
    for i in range(NY):
        before = pdbuf[0, i, own_block, :] * before + tbuf[0, i].astype(F32)
    carry = before * zh.astype(F32)
    for i in range(NY):
        cslab[i] = carry.astype(BF16)
        carry = pdbuf[zh, i, own_block, :] * carry + tbuf[zh, i].astype(F32)
    back = []
    for k in range(1, NY):
        j = lax.rem(y + k, NY)
        back.append(
            send(cslab.at[j], cbuf.at[y], c_s.at[k - 1], c_r.at[k - 1], tm_at(zh, j, x), head)
        )
    cbuf[y] = cslab[y]
    attend(1)
    take(back)
    for g in range(blocks):
        at = slice(g * HD, (g + 1) * HD)
        per_block = HD // owned
        came = cbuf[g * per_block:(g + 1) * per_block].reshape(HD, WIDE).astype(F32)
        for i in range(NX):
            came = dxbuf[i, g:g + 1, :] * came
            stslab[i, at, :] = (sx[i, at, :] + came).astype(BF16)
    states = []
    for k in (2, 1, 3):
        j = lax.rem(x + k, NX)
        states.append(
            send(stslab.at[j], sbuf.at[x], st_s.at[k - 1], st_r.at[k - 1], tm_at(zh, y, j), head)
        )
    sbuf[x] = stslab[x]

    def divide(i, _):
        rows = pl.ds(pl.multiple_of(i * ROWS, ROWS), ROWS)
        first, second = res[0, rows, :], res[1, rows, :]
        total = pltpu.roll(jnp.where(low, second, first), HD, 1)
        res[0, rows, :] = jnp.where(low, first, second) / total
        return 0

    lax.fori_loop(0, TOKS // ROWS, divide, 0)
    take(states)
    for g in range(NB):
        state = sbuf[g // blocks, (g % blocks) * HD:(g % blocks + 1) * HD, :].astype(F32)
        sbd[g * WIDE:g * WIDE + HD, :] = jnp.where(low, state, 0.0).astype(BF16)
        sbd[g * WIDE + HD:(g + 1) * WIDE, :] = jnp.where(low, 0.0, state).astype(BF16)
    sent = []
    for n, zz in enumerate((nearest[2], nearest[3], nearest[1], nearest[0])):
        rows = pl.ds(pl.multiple_of(zz * ROWS, ROWS), ROWS)
        ids = bidb[rows, :]
        c32 = cc[rows, :].astype(F32)
        spread = jnp.concatenate(
            [jnp.where(ids == float(g), c32, 0.0).astype(BF16) for g in range(NB)], axis=1
        )
        readout = jnp.dot(spread, sbd[...], preferred_element_type=F32) * (1.0 / 512.0)
        mixed = (res[0, rows, :] + readout).astype(BF16).reshape(CORES, LOCAL, WIDE)
        mslab[pl.ds(zz * CORES, CORES)] = mixed
        for to in (core, 1 - core):
            if n == LINE - 1 and to is core:
                continue
            dest = zz * CORES + to
            k = 2 * n + (0 if to is core else 1)
            sent.append(
                send(mslab.at[dest], mbuf.at[head], m_s.at[k], m_r.at[k], tm, dest)
            )
    mbuf[head] = mslab[head]
    wo_copy.wait()
    for move in started:
        if move not in sent:
            move.wait_send()
    take(sent)
    full = jnp.concatenate([mbuf[i] for i in range(HEADS_AXIS)], axis=1)
    out_ref[0] = jnp.dot(full, wo[...], preferred_element_type=F32).astype(BF16)

    for move in sent:
        move.wait_send()


def body(frames_in, in_weight, out_weight, block_ids, block_lists, decays):
    vmem = pl.BlockSpec(memory_space=pltpu.VMEM)
    dma = pltpu.SemaphoreType.DMA
    scratch = [
        pltpu.VMEM((1, LOCAL, D), BF16),
        pltpu.VMEM((16, 5 * WIDE), BF16),
        pltpu.VMEM((HEADS_AXIS, LOCAL, D), BF16),
        pltpu.VMEM((NZ, NY, NX, 16, 2 * WIDE), BF16),
        pltpu.VMEM((NZ, NY, NX, 16, 3 * WIDE), BF16),
        pltpu.VMEM((D, D), BF16),
        pltpu.VMEM((TOKS, WIDE), F32),
        pltpu.VMEM((WIDE, WIDE), BF16),
        pltpu.VMEM((2, TOKS, WIDE), BF16),
        pltpu.VMEM((2, TOKS, WIDE), BF16),
        pltpu.VMEM((2, TOKS, WIDE), BF16),
        pltpu.VMEM((TOKS, WIDE), BF16),
        pltpu.VMEM((WIDE, NB * WIDE), F32),
        pltpu.VMEM((2, TOKS, WIDE), F32),
        pltpu.VMEM((NX, 256, WIDE), BF16),
        pltpu.VMEM((NX, 256, WIDE), BF16),
        pltpu.VMEM((NX, 256, WIDE), F32),
        pltpu.VMEM((NY, 32, WIDE), BF16),
        pltpu.VMEM((NZ, NY, 32, WIDE), BF16),
        pltpu.VMEM((NY, 32, WIDE), BF16),
        pltpu.VMEM((NY, 32, WIDE), BF16),
        pltpu.VMEM((NX, 256, WIDE), BF16),
        pltpu.VMEM((NX, 256, WIDE), BF16),
        pltpu.VMEM((NB * WIDE, WIDE), BF16),
        pltpu.VMEM((HEADS_AXIS, LOCAL, WIDE), BF16),
        pltpu.VMEM((HEADS_AXIS, LOCAL, WIDE), BF16),
        pltpu.VMEM((NX, 8, WIDE), F32),
        pltpu.VMEM((NX, 8, WIDE), F32),
        pltpu.VMEM((8, WIDE), F32),
        pltpu.VMEM((NZ, NY, 8, WIDE), F32),
    ]
    for shape in (
        (2,), (2, 2, NX - 1), (2, NY - 1), (2, 2, NY // 2), (2, LINE - 1, CHUNKS),
        (2 * LINE - 1, PAIRS),
        (NX - 1,), (2, NY), (NX - 1,), (2, NY), (NY - 1,), (NX - 1,), (HEADS_AXIS,),
    ):
        scratch += [dma(shape), dma(shape)]
    scratch.append(dma((3,)))
    hbm = pl.BlockSpec(memory_space=pl.ANY)
    return pl.pallas_call(
        kernel,
        out_shape=jax.ShapeDtypeStruct((1, LOCAL, D), BF16),
        in_specs=[hbm, hbm, hbm, vmem, vmem, vmem],
        out_specs=vmem,
        scratch_shapes=scratch,
        compiler_params=pltpu.CompilerParams(
            collective_id=0, has_side_effects=True, vmem_limit_bytes=56 * 1024 * 1024
        ),
        name="layer",
    )(frames_in, in_weight, out_weight, block_ids.reshape(1, TOKS), block_lists.T, decays)


def solution(mesh):
    return jax.shard_map(
        body,
        mesh=mesh,
        in_specs=(P("tm", "head", None), P("tm", "head"), P(), P(), P(), P("tm", "head", None)),
        out_specs=P("tm", "head", None),
        check_vma=False,
    )
```

```python
import functools

import jax
import jax.numpy as jnp
from jax import lax
from jax.experimental import pallas as pl
from jax.experimental.pallas import tpu as pltpu
from jax.sharding import PartitionSpec as P

HD = 64
NB = 16
D = 1024
TOKS = 1024
LOCAL = 128
WIDE = 2 * HD
NX, NY, NZ = 4, 8, 2
NG = NY * NZ
LINE, CORES = 4, 2
HEADS_AXIS = LINE * CORES
CHUNKS = 4
PAIRS = 2
ROWS = 256
EPS = 1e-6
FAR = -256.0
F32, BF16 = jnp.float32, jnp.bfloat16
MESH = pl.DeviceIdType.MESH


class Move:
    def __init__(self, copy, go=None, come=None):
        self.copy, self.go, self.come, self.took = copy, go, come, False

    def start(self):
        self.copy.start() if self.go is None else pl.when(self.go)(self.copy.start)

    def wait_recv(self):
        self.took = True
        self.copy.wait_recv() if self.come is None else pl.when(self.come)(self.copy.wait_recv)

    def wait_send(self):
        self.copy.wait_send() if self.go is None else pl.when(self.go)(self.copy.wait_send)


def kernel(
    x_hbm, w_hbm, wo_hbm, bid_ref, lists_ref, dec_ref, out_ref,
    xin, win, xbuf, wvb, wqkc, wo, bidb, fmat, qa, ka, va, cc, acc, res,
    sslab, ubuf, sx, tslab, tbuf, cslab, cbuf, stslab, sbuf, sbd, mslab, mbuf,
    dout, dxbuf, pdout, pdbuf,
    wz_s, wz_r, wx_s, wx_r, wy_s, wy_r, xg_s, xg_r, sib_s, sib_r,
    dx_s, dx_r, pd_s, pd_r, u_s, u_r, t_s, t_r, c_s, c_r, st_s, st_r, m_s, m_r, in_sem,
):
    tm, head = lax.axis_index("tm"), lax.axis_index("head")
    x, r = lax.rem(tm, NX), lax.div(tm, NX)
    y, zh = lax.rem(r, NY), lax.div(r, NY)
    z, core = lax.div(head, CORES), lax.rem(head, CORES)

    def tm_at(zz, yy, xx):
        return (zz * NY + yy) * NX + xx

    barrier = pltpu.get_barrier_semaphore()

    def greet(tm_to, head_to):
        pl.semaphore_signal(barrier, inc=1, device_id=(tm_to, head_to), device_id_type=MESH)

    first_half, second_half = zh == 0, zh == 1
    pl.when(first_half)(lambda: greet(tm_at(1 - zh, y, x), head))
    greet(tm_at(zh, y, lax.rem(x + 2, NX)), head)
    for k in (1, NX - 1):
        greet(tm_at(zh, y, lax.rem(x + k, NX)), head)
    for k in (4, 3, 5, 2, 6, 1, 7):
        greet(tm_at(zh, lax.rem(y + k, NY), x), head)
    pl.when(z > 0)(lambda: greet(tm, head - CORES))
    pl.when(z < LINE - 1)(lambda: greet(tm, head + CORES))
    greet(tm, z * CORES + 1 - core)
    expected = 11 + zh + (z > 0).astype(jnp.int32) + (z < LINE - 1).astype(jnp.int32)

    loads = [
        pltpu.make_async_copy(src, dst, in_sem.at[i])
        for i, (src, dst) in enumerate(((w_hbm, win), (x_hbm, xin), (wo_hbm, wo)))
    ]
    for load in loads:
        load.start()
    wo_copy = loads[2]
    started = []

    def send(src, dst, ssem, rsem, tm_to, head_to, go=None, come=None):
        move = Move(
            pltpu.make_async_remote_copy(
                src_ref=src, dst_ref=dst, send_sem=ssem, recv_sem=rsem,
                device_id=(tm_to, head_to), device_id_type=MESH,
            ), go, come,
        )
        move.start()
        started.append(move)
        return move

    lane = lax.broadcasted_iota(jnp.int32, (1, WIDE), 1)
    low = lane < HD

    loads[0].wait()
    raw = [win[:, i * WIDE:(i + 1) * WIDE].astype(F32) for i in range(5)]
    swap = functools.partial(pltpu.roll, shift=HD, axis=1)
    ordered = [
        jnp.where(low, raw[1], raw[3]),
        swap(jnp.where(low, raw[4], raw[1])),
        jnp.where(low, raw[0], raw[2]),
        swap(jnp.where(low, raw[3], raw[0])),
        jnp.where(low, raw[2], raw[4]),
    ]
    for i in range(5):
        buf, col = (wvb, i) if i < 2 else (wqkc, i - 2)
        buf[zh, y, x, :, col * WIDE:(col + 1) * WIDE] = ordered[i].astype(BF16)


    def part(source, k, size=LOCAL // CHUNKS):
        return xbuf.at[source * CORES + core, pl.ds(k * size, size)]

    def is_source(zz):
        return (zz >= 0) & (zz < LINE)

    line, sib = {}, {}

    def send_line(way, s, k):
        source, to = (z - (s - 1), z + 1) if way == 0 else (z + (s - 1), z - 1)
        come = is_source(z - s if way == 0 else z + s)
        ref = part(source, k)
        line[way, s, k] = send(
            ref, ref, xg_s.at[way, s - 1, k], xg_r.at[way, s - 1, k], tm, to * CORES + core,
            is_source(source) & is_source(to), come,
        )

    def send_sib(n, source, k, go=None, come=None):
        ref = part(source, k, LOCAL // PAIRS)
        sib[n, k] = send(
            ref, ref, sib_s.at[n, k], sib_r.at[n, k], tm, z * CORES + 1 - core, go, come
        )

    def take_line(s, k):
        for way in range(2):
            move = line[way, s, k]
            move.wait_recv()
            if s < LINE - 1:
                send_line(way, s + 1, k)
            if k % (CHUNKS // PAIRS) == CHUNKS // PAIRS - 1:
                send_sib(
                    2 * s - 1 + way, z - s if way == 0 else z + s, k // (CHUNKS // PAIRS),
                    move.come, move.come,
                )

    parts = (wvb, wqkc)

    def send_z(c, go, come):
        ref = parts[c].at[zh, y, x]
        return [send(ref, ref, wz_s.at[c], wz_r.at[c], tm_at(1 - zh, y, x), head, go, come)]

    def send_x(c, side):
        ref = parts[c].at[zh if side == 0 else 1 - zh, y, x]
        return [
            send(ref, ref, wx_s.at[c, side, k - 1], wx_r.at[c, side, k - 1],
                 tm_at(zh, y, lax.rem(x + k, NX)), head)
            for k in range(1, NX)
        ]

    def take(moves):
        for move in moves:
            move.wait_recv()

    rings = {}

    def send_y(c, side):
        ref = parts[c].at[zh if side == 0 else 1 - zh, y]
        return [
            send(ref, ref, wy_s.at[c, side, k - 1], wy_r.at[c, side, k - 1],
                 tm_at(zh, lax.rem(y + k, NY), x), head)
            for k in (4, 3, 5, 2, 6, 1, 7)
        ]

    pl.semaphore_wait(barrier, expected)
    far = send_z(0, second_half, first_half)
    own = send_x(0, 0)
    loads[1].wait()
    wide = xin[0].astype(F32)
    xbuf[head] = (
        wide * lax.rsqrt(jnp.mean(wide * wide, axis=-1, keepdims=True) + EPS)
    ).astype(BF16)
    for k in range(CHUNKS):
        for way in range(2):
            send_line(way, 1, k)
    for k in range(PAIRS):
        send_sib(0, z, k)
    far_late = send_z(1, second_half, first_half)
    own_late = send_x(1, 0)
    take(own)
    direct = send_y(0, 0)

    dec = dec_ref[0]
    gi = lax.broadcasted_iota(jnp.int32, (NB, NB), 0)
    gj = lax.broadcasted_iota(jnp.int32, (NB, NB), 1)
    cols = [
        jnp.sum(jnp.where(gi == gj, dec[h:h + 1, :], 0.0), axis=1, keepdims=True) for h in range(2)
    ]
    drow = jnp.where(low, cols[0], cols[1])
    dout[...] = jnp.zeros_like(dout)
    for j in range(NX):
        dout[j, 0:4, :] = drow[4 * j:4 * j + 4, :]
    dxbuf[x] = dout[x]

    dx = []
    for k in range(1, NX):
        j = lax.rem(x + k, NX)
        dx.append(
            send(dout.at[j], dxbuf.at[x], dx_s.at[k - 1], dx_r.at[k - 1], tm_at(zh, y, j), head)
        )
    take_line(1, 0)
    take_line(1, 1)

    ids = jnp.broadcast_to(bid_ref[...].astype(F32), (WIDE, TOKS))
    for i in range(TOKS // WIDE):
        bidb[i * WIDE:(i + 1) * WIDE, :] = ids[:, i * WIDE:(i + 1) * WIDE].T
    fmat[...] = jnp.zeros_like(fmat)
    wrapped = lane & (HD - 1)
    wrapped_f = wrapped.astype(F32)
    key_block = lax.broadcasted_iota(jnp.int32, (WIDE, NB), 0) & (HD - 1)
    adjacent = key_block >= NB
    for k in range(lists_ref.shape[0]):
        adjacent = adjacent | (lists_ref[k:k + 1, :] == key_block)
    fmat[:, 0:NB] = jnp.where(adjacent, 0.0, FAR).astype(BF16)

    take_line(1, 2)
    take(own_late)
    late = send_y(1, 0)
    take_line(1, 3)
    take(dx)
    prod = dxbuf[0]
    for i in range(1, NX):
        prod = prod * dxbuf[i]
    pdout[...] = prod
    pdbuf[zh, y] = prod
    for k in range(CHUNKS):
        take_line(2, k)
    take(far)
    take(send_z(0, first_half, second_half))
    other = send_x(0, 1)
    take(far_late)
    far_late = send_z(1, first_half, second_half)
    take_line(3, 0)
    take(other)
    direct += send_y(0, 1)
    take(far_late)
    other_late = send_x(1, 1)
    take_line(3, 1)
    take(direct)
    take(other_late)
    late += send_y(1, 1)

    def to_group(src_of, dst, ssem, rsem):
        moves = []
        for k in range(NY):
            j = lax.rem(y + k, NY)
            moves.append(
                send(src_of(j), dst.at[0, y], ssem.at[1, k], rsem.at[1, k], tm_at(1, j, x), head,
                     first_half, second_half)
            )
        for k in range(1, NY):
            j = lax.rem(y + k, NY)
            moves.append(
                send(src_of(j), dst.at[zh, y], ssem.at[0, k], rsem.at[0, k], tm_at(zh, j, x), head)
            )
        return moves

    pd = to_group(lambda j: pdout, pdbuf, pd_s, pd_r)

    def project_vb(zz, first):
        rows = pl.ds(pl.multiple_of(zz * ROWS, ROWS), ROWS)
        tokens = xbuf[pl.ds(zz * CORES, CORES)].reshape(ROWS, D)
        weights = wvb[...].reshape(D, 2 * WIDE)
        p = jnp.dot(tokens, weights, preferred_element_type=F32).astype(BF16).astype(F32)
        v, b = p[:, 0:WIDE], p[:, WIDE:2 * WIDE]
        ids = bidb[rows, :]
        va[0, rows, :] = jnp.where(low, v, 1.0).astype(BF16)
        va[1, rows, :] = jnp.where(low, 1.0, v).astype(BF16)
        bt = b.T.astype(BF16)
        for g in range(0, NB, 4):
            masked = jnp.concatenate(
                [jnp.where(ids == float(g + n), v, 0.0).astype(BF16) for n in range(4)], axis=1
            )
            at = slice(g * WIDE, (g + 4) * WIDE)
            term = jnp.dot(bt, masked, preferred_element_type=F32)
            acc[:, at] = term if first else acc[:, at] + term

    odd = lax.rem(z, 2)
    nearest = (z, z + 1 - 2 * odd, lax.rem(z + 2, LINE), 3 - z)
    for n in range(LINE):
        if n == LINE - 1:
            take_line(3, 2)
            take_line(3, 3)
        for way in range(2) if n else (0,):
            for k in range(PAIRS):
                sib[2 * n - 1 + way if n else 0, k].wait_recv()
        project_vb(nearest[n], n == 0)

    for g in range(NB):
        at = slice(g * WIDE, (g + 1) * WIDE)
        both = jnp.where(low, acc[0:HD, at], acc[HD:WIDE, at])
        sslab[g // 4, (g % 4) * HD:(g % 4 + 1) * HD, :] = both.astype(BF16)
    up = []
    for k in (2, 1, 3):
        j = lax.rem(x + k, NX)
        up.append(
            send(sslab.at[j], ubuf.at[x], u_s.at[k - 1], u_r.at[k - 1], tm_at(zh, y, j), head)
        )
    ubuf[x] = sslab[x]

    def normed_heads(values):
        square = values * values
        means = [
            jnp.sum(jnp.where(keep, square, 0.0), axis=-1, keepdims=True) * (1.0 / HD)
            for keep in (low, ~low)
        ]
        return (values * lax.rsqrt(jnp.where(low, means[0], means[1]) + EPS)).astype(BF16).astype(F32)

    def project_qkc():
        tokens = xbuf[...].reshape(TOKS, D)
        weights = wqkc[...].reshape(D, 3 * WIDE)
        p = jnp.dot(tokens, weights, preferred_element_type=F32).astype(BF16)
        q, k, c = (p[:, j * WIDE:(j + 1) * WIDE] for j in range(3))
        hot = jnp.where(bidb[...] == wrapped_f, 1.0, 0.0)
        banned = lax.dot_general(
            hot.astype(BF16), fmat[...], (((1,), (1,)), ((), ())), preferred_element_type=F32
        )
        qn = normed_heads(q.astype(F32)) * 0.125
        kn = normed_heads(k.astype(F32))
        qa[0, :, :] = jnp.where(low, qn, banned).astype(BF16)
        qa[1, :, :] = jnp.where(low, banned, qn).astype(BF16)
        ka[0, :, :] = jnp.where(low, kn, hot).astype(BF16)
        ka[1, :, :] = jnp.where(low, hot, kn).astype(BF16)
        cc[...] = c

    def attend(h):
        score = lax.dot_general(
            qa[h], ka[h], (((1,), (1,)), ((), ())), preferred_element_type=F32
        )
        res[h] = jnp.dot(jnp.exp(score).astype(BF16), va[h], preferred_element_type=F32)

    take(up)
    blocks, owned = NB // NX, 32
    for g in range(blocks):
        at = slice(g * HD, (g + 1) * HD)
        state = ubuf[0, at, :].astype(F32)
        sx[0, at, :] = state
        for i in range(1, NX):
            state = dxbuf[i, g:g + 1, :] * state + ubuf[i, at, :].astype(F32)
            sx[i, at, :] = state
        for n in range(HD // owned):
            piece = state[n * owned:(n + 1) * owned, :].astype(BF16)
            tslab[g * (HD // owned) + n] = piece
    tot = to_group(lambda j: tslab.at[j], tbuf, t_s, t_r)
    tbuf[zh, y] = tslab[y]
    take(late)
    project_qkc()
    attend(0)
    take(pd)
    take(tot)
    own_block = pl.ds(lax.div(y, HD // owned), 1)
    before = jnp.zeros((owned, WIDE), F32)
    for i in range(NY):
        before = pdbuf[0, i, own_block, :] * before + tbuf[0, i].astype(F32)
    carry = before * zh.astype(F32)
    for i in range(NY):
        cslab[i] = carry.astype(BF16)
        carry = pdbuf[zh, i, own_block, :] * carry + tbuf[zh, i].astype(F32)
    back = []
    for k in range(1, NY):
        j = lax.rem(y + k, NY)
        back.append(
            send(cslab.at[j], cbuf.at[y], c_s.at[k - 1], c_r.at[k - 1], tm_at(zh, j, x), head)
        )
    cbuf[y] = cslab[y]
    attend(1)
    take(back)
    for g in range(blocks):
        at = slice(g * HD, (g + 1) * HD)
        per_block = HD // owned
        came = cbuf[g * per_block:(g + 1) * per_block].reshape(HD, WIDE).astype(F32)
        for i in range(NX):
            came = dxbuf[i, g:g + 1, :] * came
            stslab[i, at, :] = (sx[i, at, :] + came).astype(BF16)
    states = []
    for k in (2, 1, 3):
        j = lax.rem(x + k, NX)
        states.append(
            send(stslab.at[j], sbuf.at[x], st_s.at[k - 1], st_r.at[k - 1], tm_at(zh, y, j), head)
        )
    sbuf[x] = stslab[x]

    def divide(i, _):
        rows = pl.ds(pl.multiple_of(i * ROWS, ROWS), ROWS)
        first, second = res[0, rows, :], res[1, rows, :]
        total = pltpu.roll(jnp.where(low, second, first), HD, 1)
        res[0, rows, :] = jnp.where(low, first, second) / total
        return 0

    lax.fori_loop(0, TOKS // ROWS, divide, 0)
    take(states)
    for g in range(NB):
        state = sbuf[g // blocks, (g % blocks) * HD:(g % blocks + 1) * HD, :].astype(F32)
        sbd[g * WIDE:g * WIDE + HD, :] = jnp.where(low, state, 0.0).astype(BF16)
        sbd[g * WIDE + HD:(g + 1) * WIDE, :] = jnp.where(low, 0.0, state).astype(BF16)
    sent = []
    for n, zz in enumerate((nearest[2], nearest[3], nearest[1], nearest[0])):
        rows = pl.ds(pl.multiple_of(zz * ROWS, ROWS), ROWS)
        ids = bidb[rows, :]
        c32 = cc[rows, :].astype(F32)
        spread = jnp.concatenate(
            [jnp.where(ids == float(g), c32, 0.0).astype(BF16) for g in range(NB)], axis=1
        )
        readout = jnp.dot(spread, sbd[...], preferred_element_type=F32) * (1.0 / 512.0)
        mixed = (res[0, rows, :] + readout).astype(BF16).reshape(CORES, LOCAL, WIDE)
        mslab[pl.ds(zz * CORES, CORES)] = mixed
        for to in (core, 1 - core):
            if n == LINE - 1 and to is core:
                continue
            dest = zz * CORES + to
            k = 2 * n + (0 if to is core else 1)
            sent.append(
                send(mslab.at[dest], mbuf.at[head], m_s.at[k], m_r.at[k], tm, dest)
            )
    mbuf[head] = mslab[head]
    wo_copy.wait()
    for move in started:
        if move not in sent:
            move.wait_send()
    take(sent)
    full = jnp.concatenate([mbuf[i] for i in range(HEADS_AXIS)], axis=1)
    out_ref[0] = jnp.dot(full, wo[...], preferred_element_type=F32).astype(BF16)

    for move in sent:
        move.wait_send()


def body(frames_in, in_weight, out_weight, block_ids, block_lists, decays):
    vmem = pl.BlockSpec(memory_space=pltpu.VMEM)
    dma = pltpu.SemaphoreType.DMA
    scratch = [
        pltpu.VMEM((1, LOCAL, D), BF16),
        pltpu.VMEM((16, 5 * WIDE), BF16),
        pltpu.VMEM((HEADS_AXIS, LOCAL, D), BF16),
        pltpu.VMEM((NZ, NY, NX, 16, 2 * WIDE), BF16),
        pltpu.VMEM((NZ, NY, NX, 16, 3 * WIDE), BF16),
        pltpu.VMEM((D, D), BF16),
        pltpu.VMEM((TOKS, WIDE), F32),
        pltpu.VMEM((WIDE, WIDE), BF16),
        pltpu.VMEM((2, TOKS, WIDE), BF16),
        pltpu.VMEM((2, TOKS, WIDE), BF16),
        pltpu.VMEM((2, TOKS, WIDE), BF16),
        pltpu.VMEM((TOKS, WIDE), BF16),
        pltpu.VMEM((WIDE, NB * WIDE), F32),
        pltpu.VMEM((2, TOKS, WIDE), F32),
        pltpu.VMEM((NX, 256, WIDE), BF16),
        pltpu.VMEM((NX, 256, WIDE), BF16),
        pltpu.VMEM((NX, 256, WIDE), F32),
        pltpu.VMEM((NY, 32, WIDE), BF16),
        pltpu.VMEM((NZ, NY, 32, WIDE), BF16),
        pltpu.VMEM((NY, 32, WIDE), BF16),
        pltpu.VMEM((NY, 32, WIDE), BF16),
        pltpu.VMEM((NX, 256, WIDE), BF16),
        pltpu.VMEM((NX, 256, WIDE), BF16),
        pltpu.VMEM((NB * WIDE, WIDE), BF16),
        pltpu.VMEM((HEADS_AXIS, LOCAL, WIDE), BF16),
        pltpu.VMEM((HEADS_AXIS, LOCAL, WIDE), BF16),
        pltpu.VMEM((NX, 8, WIDE), F32),
        pltpu.VMEM((NX, 8, WIDE), F32),
        pltpu.VMEM((8, WIDE), F32),
        pltpu.VMEM((NZ, NY, 8, WIDE), F32),
    ]
    for shape in (
        (2,), (2, 2, NX - 1), (2, 2, NY - 1), (2, LINE - 1, CHUNKS),
        (2 * LINE - 1, PAIRS),
        (NX - 1,), (2, NY), (NX - 1,), (2, NY), (NY - 1,), (NX - 1,), (HEADS_AXIS,),
    ):
        scratch += [dma(shape), dma(shape)]
    scratch.append(dma((3,)))
    hbm = pl.BlockSpec(memory_space=pl.ANY)
    return pl.pallas_call(
        kernel,
        out_shape=jax.ShapeDtypeStruct((1, LOCAL, D), BF16),
        in_specs=[hbm, hbm, hbm, vmem, vmem, vmem],
        out_specs=vmem,
        scratch_shapes=scratch,
        compiler_params=pltpu.CompilerParams(
            collective_id=0, has_side_effects=True, vmem_limit_bytes=56 * 1024 * 1024
        ),
        name="layer",
    )(frames_in, in_weight, out_weight, block_ids.reshape(1, TOKS), block_lists.T, decays)


def solution(mesh):
    return jax.shard_map(
        body,
        mesh=mesh,
        in_specs=(P("tm", "head", None), P("tm", "head"), P(), P(), P(), P("tm", "head", None)),
        out_specs=P("tm", "head", None),
        check_vma=False,
    )
```

```python
import functools

import jax
import jax.numpy as jnp
from jax import lax
from jax.experimental import pallas as pl
from jax.experimental.pallas import tpu as pltpu
from jax.sharding import PartitionSpec as P

HD = 64
NB = 16
D = 1024
TOKS = 1024
LOCAL = 128
WIDE = 2 * HD
NX, NY, NZ = 4, 8, 2
NG = NY * NZ
LINE, CORES = 4, 2
HEADS_AXIS = LINE * CORES
CHUNKS = 4
PAIRS = 2
ROWS = 256
EPS = 1e-6
FAR = -256.0
F32, BF16 = jnp.float32, jnp.bfloat16
MESH = pl.DeviceIdType.MESH


class Move:
    def __init__(self, copy, go=None, come=None):
        self.copy, self.go, self.come, self.took = copy, go, come, False

    def start(self):
        self.copy.start() if self.go is None else pl.when(self.go)(self.copy.start)

    def wait_recv(self):
        self.took = True
        self.copy.wait_recv() if self.come is None else pl.when(self.come)(self.copy.wait_recv)

    def wait_send(self):
        self.copy.wait_send() if self.go is None else pl.when(self.go)(self.copy.wait_send)


def kernel(
    x_hbm, w_hbm, wo_hbm, bid_ref, lists_ref, dec_ref, out_ref,
    xin, win, xbuf, wvb, wqkc, wo, bidb, fmat, qa, ka, va, cc, acc, res,
    sslab, ubuf, sx, tslab, tbuf, cslab, cbuf, stslab, sbuf, sbd, mslab, mbuf,
    dout, dxbuf, pdout, pdbuf,
    wz_s, wz_r, wx_s, wx_r, wy_s, wy_r, xg_s, xg_r, sib_s, sib_r,
    dx_s, dx_r, pd_s, pd_r, u_s, u_r, t_s, t_r, c_s, c_r, st_s, st_r, m_s, m_r, in_sem,
):
    tm, head = lax.axis_index("tm"), lax.axis_index("head")
    x, r = lax.rem(tm, NX), lax.div(tm, NX)
    y, zh = lax.rem(r, NY), lax.div(r, NY)
    z, core = lax.div(head, CORES), lax.rem(head, CORES)

    def tm_at(zz, yy, xx):
        return (zz * NY + yy) * NX + xx

    barrier = pltpu.get_barrier_semaphore()

    def greet(tm_to, head_to):
        pl.semaphore_signal(barrier, inc=1, device_id=(tm_to, head_to), device_id_type=MESH)

    first_half, second_half = zh == 0, zh == 1
    pl.when(first_half)(lambda: greet(tm_at(1 - zh, y, x), head))
    greet(tm_at(zh, y, lax.rem(x + 2, NX)), head)
    for k in (1, NX - 1):
        greet(tm_at(zh, y, lax.rem(x + k, NX)), head)
    for k in (4, 3, 5, 2, 6, 1, 7):
        greet(tm_at(zh, lax.rem(y + k, NY), x), head)
    pl.when(z > 0)(lambda: greet(tm, head - CORES))
    pl.when(z < LINE - 1)(lambda: greet(tm, head + CORES))
    greet(tm, z * CORES + 1 - core)
    expected = 11 + zh + (z > 0).astype(jnp.int32) + (z < LINE - 1).astype(jnp.int32)

    loads = [
        pltpu.make_async_copy(src, dst, in_sem.at[i])
        for i, (src, dst) in enumerate(((w_hbm, win), (x_hbm, xin), (wo_hbm, wo)))
    ]
    for load in loads:
        load.start()
    wo_copy = loads[2]
    started = []

    def send(src, dst, ssem, rsem, tm_to, head_to, go=None, come=None):
        move = Move(
            pltpu.make_async_remote_copy(
                src_ref=src, dst_ref=dst, send_sem=ssem, recv_sem=rsem,
                device_id=(tm_to, head_to), device_id_type=MESH,
            ), go, come,
        )
        move.start()
        started.append(move)
        return move

    lane = lax.broadcasted_iota(jnp.int32, (1, WIDE), 1)
    low = lane < HD

    loads[0].wait()
    raw = [win[:, i * WIDE:(i + 1) * WIDE].astype(F32) for i in range(5)]
    swap = functools.partial(pltpu.roll, shift=HD, axis=1)
    ordered = [
        jnp.where(low, raw[1], raw[3]),
        swap(jnp.where(low, raw[4], raw[1])),
        jnp.where(low, raw[0], raw[2]),
        swap(jnp.where(low, raw[3], raw[0])),
        jnp.where(low, raw[2], raw[4]),
    ]
    for i in range(5):
        buf, col = (wvb, i) if i < 2 else (wqkc, i - 2)
        buf[zh, y, x, :, col * WIDE:(col + 1) * WIDE] = ordered[i].astype(BF16)


    def part(source, k, size=LOCAL // CHUNKS):
        return xbuf.at[source * CORES + core, pl.ds(k * size, size)]

    def is_source(zz):
        return (zz >= 0) & (zz < LINE)

    line, sib = {}, {}

    def send_line(way, s, k):
        source, to = (z - (s - 1), z + 1) if way == 0 else (z + (s - 1), z - 1)
        come = is_source(z - s if way == 0 else z + s)
        ref = part(source, k)
        line[way, s, k] = send(
            ref, ref, xg_s.at[way, s - 1, k], xg_r.at[way, s - 1, k], tm, to * CORES + core,
            is_source(source) & is_source(to), come,
        )

    def send_sib(n, source, k, go=None, come=None):
        ref = part(source, k, LOCAL // PAIRS)
        sib[n, k] = send(
            ref, ref, sib_s.at[n, k], sib_r.at[n, k], tm, z * CORES + 1 - core, go, come
        )

    def take_line(s, k):
        for way in range(2):
            move = line[way, s, k]
            move.wait_recv()
            if s < LINE - 1:
                send_line(way, s + 1, k)
            if k % (CHUNKS // PAIRS) == CHUNKS // PAIRS - 1:
                send_sib(
                    2 * s - 1 + way, z - s if way == 0 else z + s, k // (CHUNKS // PAIRS),
                    move.come, move.come,
                )

    parts = (wvb, wqkc)

    def send_z(c, go, come):
        ref = parts[c].at[zh, y, x]
        return [send(ref, ref, wz_s.at[c], wz_r.at[c], tm_at(1 - zh, y, x), head, go, come)]

    def send_piece(c, side):
        ref = parts[c].at[zh if side == 0 else 1 - zh, y, x]
        return [
            send(ref, ref, wy_s.at[c, side, k - 1], wy_r.at[c, side, k - 1],
                 tm_at(zh, lax.rem(y + k, NY), x), head)
            for k in (4, 3, 5, 2, 6, 1, 7)
        ]

    def take(moves):
        for move in moves:
            move.wait_recv()

    def send_bulk(c, side):
        ref = parts[c].at[zh if side == 0 else 1 - zh, :, x]
        return [
            send(ref, ref, wx_s.at[c, side, k - 1], wx_r.at[c, side, k - 1],
                 tm_at(zh, y, lax.rem(x + k, NX)), head)
            for k in (2, 1, 3)
        ]

    pl.semaphore_wait(barrier, expected)
    far = send_z(0, second_half, first_half)
    own = send_piece(0, 0)
    loads[1].wait()
    wide = xin[0].astype(F32)
    xbuf[head] = (
        wide * lax.rsqrt(jnp.mean(wide * wide, axis=-1, keepdims=True) + EPS)
    ).astype(BF16)
    for k in range(CHUNKS):
        for way in range(2):
            send_line(way, 1, k)
    for k in range(PAIRS):
        send_sib(0, z, k)
    far_late = send_z(1, second_half, first_half)
    own_late = send_piece(1, 0)
    take(own)
    direct = send_bulk(0, 0)

    dec = dec_ref[0]
    gi = lax.broadcasted_iota(jnp.int32, (NB, NB), 0)
    gj = lax.broadcasted_iota(jnp.int32, (NB, NB), 1)
    cols = [
        jnp.sum(jnp.where(gi == gj, dec[h:h + 1, :], 0.0), axis=1, keepdims=True) for h in range(2)
    ]
    drow = jnp.where(low, cols[0], cols[1])
    dout[...] = jnp.zeros_like(dout)
    for j in range(NX):
        dout[j, 0:4, :] = drow[4 * j:4 * j + 4, :]
    dxbuf[x] = dout[x]

    dx = []
    for k in range(1, NX):
        j = lax.rem(x + k, NX)
        dx.append(
            send(dout.at[j], dxbuf.at[x], dx_s.at[k - 1], dx_r.at[k - 1], tm_at(zh, y, j), head)
        )
    take_line(1, 0)
    take_line(1, 1)

    ids = jnp.broadcast_to(bid_ref[...].astype(F32), (WIDE, TOKS))
    for i in range(TOKS // WIDE):
        bidb[i * WIDE:(i + 1) * WIDE, :] = ids[:, i * WIDE:(i + 1) * WIDE].T
    fmat[...] = jnp.zeros_like(fmat)
    wrapped = lane & (HD - 1)
    wrapped_f = wrapped.astype(F32)
    key_block = lax.broadcasted_iota(jnp.int32, (WIDE, NB), 0) & (HD - 1)
    adjacent = key_block >= NB
    for k in range(lists_ref.shape[0]):
        adjacent = adjacent | (lists_ref[k:k + 1, :] == key_block)
    fmat[:, 0:NB] = jnp.where(adjacent, 0.0, FAR).astype(BF16)

    take_line(1, 2)
    take(own_late)
    late = send_bulk(1, 0)
    take_line(1, 3)
    take(dx)
    prod = dxbuf[0]
    for i in range(1, NX):
        prod = prod * dxbuf[i]
    pdout[...] = prod
    pdbuf[zh, y] = prod
    for k in range(CHUNKS):
        take_line(2, k)
    take(far)
    take(send_z(0, first_half, second_half))
    other = send_piece(0, 1)
    take(far_late)
    far_late = send_z(1, first_half, second_half)
    take_line(3, 0)
    take(other)
    direct += send_bulk(0, 1)
    take(far_late)
    other_late = send_piece(1, 1)
    take_line(3, 1)
    take(direct)
    take(other_late)
    late += send_bulk(1, 1)

    def to_group(src_of, dst, ssem, rsem):
        moves = []
        for k in range(NY):
            j = lax.rem(y + k, NY)
            moves.append(
                send(src_of(j), dst.at[0, y], ssem.at[1, k], rsem.at[1, k], tm_at(1, j, x), head,
                     first_half, second_half)
            )
        for k in range(1, NY):
            j = lax.rem(y + k, NY)
            moves.append(
                send(src_of(j), dst.at[zh, y], ssem.at[0, k], rsem.at[0, k], tm_at(zh, j, x), head)
            )
        return moves

    pd = to_group(lambda j: pdout, pdbuf, pd_s, pd_r)

    def project_vb(zz, first):
        rows = pl.ds(pl.multiple_of(zz * ROWS, ROWS), ROWS)
        tokens = xbuf[pl.ds(zz * CORES, CORES)].reshape(ROWS, D)
        weights = wvb[...].reshape(D, 2 * WIDE)
        p = jnp.dot(tokens, weights, preferred_element_type=F32).astype(BF16).astype(F32)
        v, b = p[:, 0:WIDE], p[:, WIDE:2 * WIDE]
        ids = bidb[rows, :]
        va[0, rows, :] = jnp.where(low, v, 1.0).astype(BF16)
        va[1, rows, :] = jnp.where(low, 1.0, v).astype(BF16)
        bt = b.T.astype(BF16)
        for g in range(0, NB, 4):
            masked = jnp.concatenate(
                [jnp.where(ids == float(g + n), v, 0.0).astype(BF16) for n in range(4)], axis=1
            )
            at = slice(g * WIDE, (g + 4) * WIDE)
            term = jnp.dot(bt, masked, preferred_element_type=F32)
            acc[:, at] = term if first else acc[:, at] + term

    odd = lax.rem(z, 2)
    nearest = (z, z + 1 - 2 * odd, lax.rem(z + 2, LINE), 3 - z)
    for n in range(LINE):
        if n == LINE - 1:
            take_line(3, 2)
            take_line(3, 3)
        for way in range(2) if n else (0,):
            for k in range(PAIRS):
                sib[2 * n - 1 + way if n else 0, k].wait_recv()
        project_vb(nearest[n], n == 0)

    for g in range(NB):
        at = slice(g * WIDE, (g + 1) * WIDE)
        both = jnp.where(low, acc[0:HD, at], acc[HD:WIDE, at])
        sslab[g // 4, (g % 4) * HD:(g % 4 + 1) * HD, :] = both.astype(BF16)
    up = []
    for k in (2, 1, 3):
        j = lax.rem(x + k, NX)
        up.append(
            send(sslab.at[j], ubuf.at[x], u_s.at[k - 1], u_r.at[k - 1], tm_at(zh, y, j), head)
        )
    ubuf[x] = sslab[x]

    def normed_heads(values):
        square = values * values
        means = [
            jnp.sum(jnp.where(keep, square, 0.0), axis=-1, keepdims=True) * (1.0 / HD)
            for keep in (low, ~low)
        ]
        return (values * lax.rsqrt(jnp.where(low, means[0], means[1]) + EPS)).astype(BF16).astype(F32)

    def project_qkc():
        tokens = xbuf[...].reshape(TOKS, D)
        weights = wqkc[...].reshape(D, 3 * WIDE)
        p = jnp.dot(tokens, weights, preferred_element_type=F32).astype(BF16)
        q, k, c = (p[:, j * WIDE:(j + 1) * WIDE] for j in range(3))
        hot = jnp.where(bidb[...] == wrapped_f, 1.0, 0.0)
        banned = lax.dot_general(
            hot.astype(BF16), fmat[...], (((1,), (1,)), ((), ())), preferred_element_type=F32
        )
        qn = normed_heads(q.astype(F32)) * 0.125
        kn = normed_heads(k.astype(F32))
        qa[0, :, :] = jnp.where(low, qn, banned).astype(BF16)
        qa[1, :, :] = jnp.where(low, banned, qn).astype(BF16)
        ka[0, :, :] = jnp.where(low, kn, hot).astype(BF16)
        ka[1, :, :] = jnp.where(low, hot, kn).astype(BF16)
        cc[...] = c

    def attend(h):
        score = lax.dot_general(
            qa[h], ka[h], (((1,), (1,)), ((), ())), preferred_element_type=F32
        )
        res[h] = jnp.dot(jnp.exp(score).astype(BF16), va[h], preferred_element_type=F32)

    take(up)
    blocks, owned = NB // NX, 32
    for g in range(blocks):
        at = slice(g * HD, (g + 1) * HD)
        state = ubuf[0, at, :].astype(F32)
        sx[0, at, :] = state
        for i in range(1, NX):
            state = dxbuf[i, g:g + 1, :] * state + ubuf[i, at, :].astype(F32)
            sx[i, at, :] = state
        for n in range(HD // owned):
            piece = state[n * owned:(n + 1) * owned, :].astype(BF16)
            tslab[g * (HD // owned) + n] = piece
    tot = to_group(lambda j: tslab.at[j], tbuf, t_s, t_r)
    tbuf[zh, y] = tslab[y]
    take(late)
    project_qkc()
    attend(0)
    take(pd)
    take(tot)
    own_block = pl.ds(lax.div(y, HD // owned), 1)
    before = jnp.zeros((owned, WIDE), F32)
    for i in range(NY):
        before = pdbuf[0, i, own_block, :] * before + tbuf[0, i].astype(F32)
    carry = before * zh.astype(F32)
    for i in range(NY):
        cslab[i] = carry.astype(BF16)
        carry = pdbuf[zh, i, own_block, :] * carry + tbuf[zh, i].astype(F32)
    back = []
    for k in range(1, NY):
        j = lax.rem(y + k, NY)
        back.append(
            send(cslab.at[j], cbuf.at[y], c_s.at[k - 1], c_r.at[k - 1], tm_at(zh, j, x), head)
        )
    cbuf[y] = cslab[y]
    attend(1)
    take(back)
    for g in range(blocks):
        at = slice(g * HD, (g + 1) * HD)
        per_block = HD // owned
        came = cbuf[g * per_block:(g + 1) * per_block].reshape(HD, WIDE).astype(F32)
        for i in range(NX):
            came = dxbuf[i, g:g + 1, :] * came
            stslab[i, at, :] = (sx[i, at, :] + came).astype(BF16)
    states = []
    for k in (2, 1, 3):
        j = lax.rem(x + k, NX)
        states.append(
            send(stslab.at[j], sbuf.at[x], st_s.at[k - 1], st_r.at[k - 1], tm_at(zh, y, j), head)
        )
    sbuf[x] = stslab[x]

    def divide(i, _):
        rows = pl.ds(pl.multiple_of(i * ROWS, ROWS), ROWS)
        first, second = res[0, rows, :], res[1, rows, :]
        total = pltpu.roll(jnp.where(low, second, first), HD, 1)
        res[0, rows, :] = jnp.where(low, first, second) / total
        return 0

    lax.fori_loop(0, TOKS // ROWS, divide, 0)
    take(states)
    for g in range(NB):
        state = sbuf[g // blocks, (g % blocks) * HD:(g % blocks + 1) * HD, :].astype(F32)
        sbd[g * WIDE:g * WIDE + HD, :] = jnp.where(low, state, 0.0).astype(BF16)
        sbd[g * WIDE + HD:(g + 1) * WIDE, :] = jnp.where(low, 0.0, state).astype(BF16)
    sent = []
    for n, zz in enumerate((nearest[2], nearest[3], nearest[1], nearest[0])):
        rows = pl.ds(pl.multiple_of(zz * ROWS, ROWS), ROWS)
        ids = bidb[rows, :]
        c32 = cc[rows, :].astype(F32)
        spread = jnp.concatenate(
            [jnp.where(ids == float(g), c32, 0.0).astype(BF16) for g in range(NB)], axis=1
        )
        readout = jnp.dot(spread, sbd[...], preferred_element_type=F32) * (1.0 / 512.0)
        mixed = (res[0, rows, :] + readout).astype(BF16).reshape(CORES, LOCAL, WIDE)
        mslab[pl.ds(zz * CORES, CORES)] = mixed
        for to in (core, 1 - core):
            if n == LINE - 1 and to is core:
                continue
            dest = zz * CORES + to
            k = 2 * n + (0 if to is core else 1)
            sent.append(
                send(mslab.at[dest], mbuf.at[head], m_s.at[k], m_r.at[k], tm, dest)
            )
    mbuf[head] = mslab[head]
    wo_copy.wait()
    for move in started:
        if move not in sent:
            move.wait_send()
    take(sent)
    full = jnp.concatenate([mbuf[i] for i in range(HEADS_AXIS)], axis=1)
    out_ref[0] = jnp.dot(full, wo[...], preferred_element_type=F32).astype(BF16)

    for move in sent:
        move.wait_send()


def body(frames_in, in_weight, out_weight, block_ids, block_lists, decays):
    vmem = pl.BlockSpec(memory_space=pltpu.VMEM)
    dma = pltpu.SemaphoreType.DMA
    scratch = [
        pltpu.VMEM((1, LOCAL, D), BF16),
        pltpu.VMEM((16, 5 * WIDE), BF16),
        pltpu.VMEM((HEADS_AXIS, LOCAL, D), BF16),
        pltpu.VMEM((NZ, NY, NX, 16, 2 * WIDE), BF16),
        pltpu.VMEM((NZ, NY, NX, 16, 3 * WIDE), BF16),
        pltpu.VMEM((D, D), BF16),
        pltpu.VMEM((TOKS, WIDE), F32),
        pltpu.VMEM((WIDE, WIDE), BF16),
        pltpu.VMEM((2, TOKS, WIDE), BF16),
        pltpu.VMEM((2, TOKS, WIDE), BF16),
        pltpu.VMEM((2, TOKS, WIDE), BF16),
        pltpu.VMEM((TOKS, WIDE), BF16),
        pltpu.VMEM((WIDE, NB * WIDE), F32),
        pltpu.VMEM((2, TOKS, WIDE), F32),
        pltpu.VMEM((NX, 256, WIDE), BF16),
        pltpu.VMEM((NX, 256, WIDE), BF16),
        pltpu.VMEM((NX, 256, WIDE), F32),
        pltpu.VMEM((NY, 32, WIDE), BF16),
        pltpu.VMEM((NZ, NY, 32, WIDE), BF16),
        pltpu.VMEM((NY, 32, WIDE), BF16),
        pltpu.VMEM((NY, 32, WIDE), BF16),
        pltpu.VMEM((NX, 256, WIDE), BF16),
        pltpu.VMEM((NX, 256, WIDE), BF16),
        pltpu.VMEM((NB * WIDE, WIDE), BF16),
        pltpu.VMEM((HEADS_AXIS, LOCAL, WIDE), BF16),
        pltpu.VMEM((HEADS_AXIS, LOCAL, WIDE), BF16),
        pltpu.VMEM((NX, 8, WIDE), F32),
        pltpu.VMEM((NX, 8, WIDE), F32),
        pltpu.VMEM((8, WIDE), F32),
        pltpu.VMEM((NZ, NY, 8, WIDE), F32),
    ]
    for shape in (
        (2,), (2, 2, NX - 1), (2, 2, NY - 1), (2, LINE - 1, CHUNKS),
        (2 * LINE - 1, PAIRS),
        (NX - 1,), (2, NY), (NX - 1,), (2, NY), (NY - 1,), (NX - 1,), (HEADS_AXIS,),
    ):
        scratch += [dma(shape), dma(shape)]
    scratch.append(dma((3,)))
    hbm = pl.BlockSpec(memory_space=pl.ANY)
    return pl.pallas_call(
        kernel,
        out_shape=jax.ShapeDtypeStruct((1, LOCAL, D), BF16),
        in_specs=[hbm, hbm, hbm, vmem, vmem, vmem],
        out_specs=vmem,
        scratch_shapes=scratch,
        compiler_params=pltpu.CompilerParams(
            collective_id=0, has_side_effects=True, vmem_limit_bytes=56 * 1024 * 1024
        ),
        name="layer",
    )(frames_in, in_weight, out_weight, block_ids.reshape(1, TOKS), block_lists.T, decays)


def solution(mesh):
    return jax.shard_map(
        body,
        mesh=mesh,
        in_specs=(P("tm", "head", None), P("tm", "head"), P(), P(), P(), P("tm", "head", None)),
        out_specs=P("tm", "head", None),
        check_vma=False,
    )
```

```python
import functools

import jax
import jax.numpy as jnp
from jax import lax
from jax.experimental import pallas as pl
from jax.experimental.pallas import tpu as pltpu
from jax.sharding import PartitionSpec as P

HD = 64
NB = 16
D = 1024
TOKS = 1024
LOCAL = 128
WIDE = 2 * HD
NX, NY, NZ = 4, 8, 2
NG = NY * NZ
LINE, CORES = 4, 2
HEADS_AXIS = LINE * CORES
CHUNKS = 4
PAIRS = 2
ROWS = 256
EPS = 1e-6
FAR = -256.0
F32, BF16 = jnp.float32, jnp.bfloat16
MESH = pl.DeviceIdType.MESH


class Move:
    def __init__(self, copy, go=None, come=None):
        self.copy, self.go, self.come, self.took = copy, go, come, False

    def start(self):
        self.copy.start() if self.go is None else pl.when(self.go)(self.copy.start)

    def wait_recv(self):
        self.took = True
        self.copy.wait_recv() if self.come is None else pl.when(self.come)(self.copy.wait_recv)

    def wait_send(self):
        self.copy.wait_send() if self.go is None else pl.when(self.go)(self.copy.wait_send)


def kernel(
    x_hbm, w_hbm, wo_hbm, bid_ref, lists_ref, dec_ref, out_ref,
    xin, win, xbuf, wvb, wqkc, wo, bidb, fmat, qa, ka, va, cc, acc, res,
    sslab, ubuf, sx, tslab, tbuf, cslab, cbuf, stslab, sbuf, sbd, mslab, mbuf,
    dout, dxbuf, pdout, pdbuf,
    wz_s, wz_r, wx_s, wx_r, wy_s, wy_r, xg_s, xg_r, sib_s, sib_r,
    dx_s, dx_r, pd_s, pd_r, u_s, u_r, t_s, t_r, c_s, c_r, st_s, st_r, m_s, m_r, in_sem,
):
    tm, head = lax.axis_index("tm"), lax.axis_index("head")
    x, r = lax.rem(tm, NX), lax.div(tm, NX)
    y, zh = lax.rem(r, NY), lax.div(r, NY)
    z, core = lax.div(head, CORES), lax.rem(head, CORES)

    def tm_at(zz, yy, xx):
        return (zz * NY + yy) * NX + xx

    barrier = pltpu.get_barrier_semaphore()

    def greet(tm_to, head_to):
        pl.semaphore_signal(barrier, inc=1, device_id=(tm_to, head_to), device_id_type=MESH)

    first_half, second_half = zh == 0, zh == 1
    pl.when(first_half)(lambda: greet(tm_at(1 - zh, y, x), head))
    greet(tm_at(zh, y, lax.rem(x + 2, NX)), head)
    for k in (1, NX - 1):
        greet(tm_at(zh, y, lax.rem(x + k, NX)), head)
    for k in (4, 3, 5, 2, 6, 1, 7):
        greet(tm_at(zh, lax.rem(y + k, NY), x), head)
    pl.when(z > 0)(lambda: greet(tm, head - CORES))
    pl.when(z < LINE - 1)(lambda: greet(tm, head + CORES))
    greet(tm, z * CORES + 1 - core)
    expected = 11 + zh + (z > 0).astype(jnp.int32) + (z < LINE - 1).astype(jnp.int32)

    loads = [
        pltpu.make_async_copy(src, dst, in_sem.at[i])
        for i, (src, dst) in enumerate(((w_hbm, win), (x_hbm, xin), (wo_hbm, wo)))
    ]
    for load in loads:
        load.start()
    wo_copy = loads[2]
    started = []

    def send(src, dst, ssem, rsem, tm_to, head_to, go=None, come=None):
        move = Move(
            pltpu.make_async_remote_copy(
                src_ref=src, dst_ref=dst, send_sem=ssem, recv_sem=rsem,
                device_id=(tm_to, head_to), device_id_type=MESH,
            ), go, come,
        )
        move.start()
        started.append(move)
        return move

    lane = lax.broadcasted_iota(jnp.int32, (1, WIDE), 1)
    low = lane < HD

    loads[0].wait()
    raw = [win[:, i * WIDE:(i + 1) * WIDE].astype(F32) for i in range(5)]
    swap = functools.partial(pltpu.roll, shift=HD, axis=1)
    ordered = [
        jnp.where(low, raw[1], raw[3]),
        swap(jnp.where(low, raw[4], raw[1])),
        jnp.where(low, raw[0], raw[2]),
        swap(jnp.where(low, raw[3], raw[0])),
        jnp.where(low, raw[2], raw[4]),
    ]
    for i in range(5):
        buf, col = (wvb, i) if i < 2 else (wqkc, i - 2)
        buf[zh, y, x, :, col * WIDE:(col + 1) * WIDE] = ordered[i].astype(BF16)


    def part(source, k, size=LOCAL // CHUNKS):
        return xbuf.at[source * CORES + core, pl.ds(k * size, size)]

    def is_source(zz):
        return (zz >= 0) & (zz < LINE)

    line, sib = {}, {}

    def send_line(way, s, k):
        source, to = (z - (s - 1), z + 1) if way == 0 else (z + (s - 1), z - 1)
        come = is_source(z - s if way == 0 else z + s)
        ref = part(source, k)
        line[way, s, k] = send(
            ref, ref, xg_s.at[way, s - 1, k], xg_r.at[way, s - 1, k], tm, to * CORES + core,
            is_source(source) & is_source(to), come,
        )

    def send_sib(n, source, k, go=None, come=None):
        ref = part(source, k, LOCAL // PAIRS)
        sib[n, k] = send(
            ref, ref, sib_s.at[n, k], sib_r.at[n, k], tm, z * CORES + 1 - core, go, come
        )

    def take_line(s, k):
        for way in range(2):
            move = line[way, s, k]
            move.wait_recv()
            if s < LINE - 1:
                send_line(way, s + 1, k)
            if k % (CHUNKS // PAIRS) == CHUNKS // PAIRS - 1:
                send_sib(
                    2 * s - 1 + way, z - s if way == 0 else z + s, k // (CHUNKS // PAIRS),
                    move.come, move.come,
                )

    parts = (wvb, wqkc)

    def send_z(c, go, come):
        ref = parts[c].at[zh, y, x]
        return [send(ref, ref, wz_s.at[c], wz_r.at[c], tm_at(1 - zh, y, x), head, go, come)]

    def send_piece(c, side):
        ref = parts[c].at[zh if side == 0 else 1 - zh, y, x]
        return [
            send(ref, ref, wy_s.at[c, side, k - 1], wy_r.at[c, side, k - 1],
                 tm_at(zh, lax.rem(y + k, NY), x), head)
            for k in (4, 3, 5, 2, 6, 1, 7)
        ]

    def take(moves):
        for move in moves:
            move.wait_recv()

    def send_bulk(c, side):
        ref = parts[c].at[zh if side == 0 else 1 - zh, :, x]
        return [
            send(ref, ref, wx_s.at[c, side, k - 1], wx_r.at[c, side, k - 1],
                 tm_at(zh, y, lax.rem(x + k, NX)), head)
            for k in (2, 1, 3)
        ]

    pl.semaphore_wait(barrier, expected)
    far = send_z(0, second_half, first_half)
    own = send_piece(0, 0)
    loads[1].wait()
    wide = xin[0].astype(F32)
    xbuf[head] = (
        wide * lax.rsqrt(jnp.mean(wide * wide, axis=-1, keepdims=True) + EPS)
    ).astype(BF16)
    for k in range(CHUNKS):
        for way in range(2):
            send_line(way, 1, k)
    for k in range(PAIRS):
        send_sib(0, z, k)
    far_late = send_z(1, second_half, first_half)
    own_late = send_piece(1, 0)
    take(own)
    direct = send_bulk(0, 0)

    dec = dec_ref[0]
    gi = lax.broadcasted_iota(jnp.int32, (NB, NB), 0)
    gj = lax.broadcasted_iota(jnp.int32, (NB, NB), 1)
    cols = [
        jnp.sum(jnp.where(gi == gj, dec[h:h + 1, :], 0.0), axis=1, keepdims=True) for h in range(2)
    ]
    drow = jnp.where(low, cols[0], cols[1])
    dout[...] = jnp.zeros_like(dout)
    for j in range(NX):
        dout[j, 0:4, :] = drow[4 * j:4 * j + 4, :]
    dxbuf[x] = dout[x]

    dx = []
    for k in range(1, NX):
        j = lax.rem(x + k, NX)
        dx.append(
            send(dout.at[j], dxbuf.at[x], dx_s.at[k - 1], dx_r.at[k - 1], tm_at(zh, y, j), head)
        )
    take_line(1, 0)
    take_line(1, 1)

    ids = jnp.broadcast_to(bid_ref[...].astype(F32), (WIDE, TOKS))
    for i in range(TOKS // WIDE):
        bidb[i * WIDE:(i + 1) * WIDE, :] = ids[:, i * WIDE:(i + 1) * WIDE].T
    fmat[...] = jnp.zeros_like(fmat)
    wrapped = lane & (HD - 1)
    wrapped_f = wrapped.astype(F32)
    key_block = lax.broadcasted_iota(jnp.int32, (WIDE, NB), 0) & (HD - 1)
    adjacent = key_block >= NB
    for k in range(lists_ref.shape[0]):
        adjacent = adjacent | (lists_ref[k:k + 1, :] == key_block)
    fmat[:, 0:NB] = jnp.where(adjacent, 0.0, FAR).astype(BF16)

    take_line(1, 2)
    take(own_late)
    late = send_bulk(1, 0)
    take_line(1, 3)
    take(dx)
    prod = dxbuf[0]
    for i in range(1, NX):
        prod = prod * dxbuf[i]
    pdout[...] = prod
    pdbuf[zh, y] = prod
    for k in range(CHUNKS):
        take_line(2, k)
    take(far)
    take(send_z(0, first_half, second_half))
    other = send_piece(0, 1)
    take(far_late)
    far_late = send_z(1, first_half, second_half)
    take_line(3, 0)
    take(other)
    direct += send_bulk(0, 1)
    take(far_late)
    other_late = send_piece(1, 1)
    take_line(3, 1)
    take(direct)
    take(other_late)
    late += send_bulk(1, 1)

    def to_group(src_of, dst, ssem, rsem):
        moves = []
        for k in range(NY):
            j = lax.rem(y + k, NY)
            moves.append(
                send(src_of(j), dst.at[0, y], ssem.at[1, k], rsem.at[1, k], tm_at(1, j, x), head,
                     first_half, second_half)
            )
        for k in range(1, NY):
            j = lax.rem(y + k, NY)
            moves.append(
                send(src_of(j), dst.at[zh, y], ssem.at[0, k], rsem.at[0, k], tm_at(zh, j, x), head)
            )
        return moves

    def project_vb(zz, first):
        rows = pl.ds(pl.multiple_of(zz * ROWS, ROWS), ROWS)
        tokens = xbuf[pl.ds(zz * CORES, CORES)].reshape(ROWS, D)
        weights = wvb[...].reshape(D, 2 * WIDE)
        p = jnp.dot(tokens, weights, preferred_element_type=F32).astype(BF16).astype(F32)
        v, b = p[:, 0:WIDE], p[:, WIDE:2 * WIDE]
        ids = bidb[rows, :]
        va[0, rows, :] = jnp.where(low, v, 1.0).astype(BF16)
        va[1, rows, :] = jnp.where(low, 1.0, v).astype(BF16)
        bt = b.T.astype(BF16)
        for g in range(0, NB, 4):
            masked = jnp.concatenate(
                [jnp.where(ids == float(g + n), v, 0.0).astype(BF16) for n in range(4)], axis=1
            )
            at = slice(g * WIDE, (g + 4) * WIDE)
            term = jnp.dot(bt, masked, preferred_element_type=F32)
            acc[:, at] = term if first else acc[:, at] + term

    odd = lax.rem(z, 2)
    nearest = (z, z + 1 - 2 * odd, lax.rem(z + 2, LINE), 3 - z)
    for n in range(LINE):
        if 0 < n < LINE - 1:
            take_line(3, n + 1)
        for way in range(2) if n else (0,):
            for k in range(PAIRS):
                sib[2 * n - 1 + way if n else 0, k].wait_recv()
        project_vb(nearest[n], n == 0)

    for g in range(NB):
        at = slice(g * WIDE, (g + 1) * WIDE)
        both = jnp.where(low, acc[0:HD, at], acc[HD:WIDE, at])
        sslab[g // 4, (g % 4) * HD:(g % 4 + 1) * HD, :] = both.astype(BF16)
    up = []
    for k in (2, 1, 3):
        j = lax.rem(x + k, NX)
        up.append(
            send(sslab.at[j], ubuf.at[x], u_s.at[k - 1], u_r.at[k - 1], tm_at(zh, y, j), head)
        )
    ubuf[x] = sslab[x]
    pd = to_group(lambda j: pdout, pdbuf, pd_s, pd_r)

    def normed_heads(values):
        square = values * values
        means = [
            jnp.sum(jnp.where(keep, square, 0.0), axis=-1, keepdims=True) * (1.0 / HD)
            for keep in (low, ~low)
        ]
        return (values * lax.rsqrt(jnp.where(low, means[0], means[1]) + EPS)).astype(BF16).astype(F32)

    def project_qkc():
        tokens = xbuf[...].reshape(TOKS, D)
        weights = wqkc[...].reshape(D, 3 * WIDE)
        p = jnp.dot(tokens, weights, preferred_element_type=F32).astype(BF16)
        q, k, c = (p[:, j * WIDE:(j + 1) * WIDE] for j in range(3))
        hot = jnp.where(bidb[...] == wrapped_f, 1.0, 0.0)
        banned = lax.dot_general(
            hot.astype(BF16), fmat[...], (((1,), (1,)), ((), ())), preferred_element_type=F32
        )
        qn = normed_heads(q.astype(F32)) * 0.125
        kn = normed_heads(k.astype(F32))
        qa[0, :, :] = jnp.where(low, qn, banned).astype(BF16)
        qa[1, :, :] = jnp.where(low, banned, qn).astype(BF16)
        ka[0, :, :] = jnp.where(low, kn, hot).astype(BF16)
        ka[1, :, :] = jnp.where(low, hot, kn).astype(BF16)
        cc[...] = c

    def attend(h):
        score = lax.dot_general(
            qa[h], ka[h], (((1,), (1,)), ((), ())), preferred_element_type=F32
        )
        res[h] = jnp.dot(jnp.exp(score).astype(BF16), va[h], preferred_element_type=F32)

    take(up)
    blocks, owned = NB // NX, 32
    for g in range(blocks):
        at = slice(g * HD, (g + 1) * HD)
        state = ubuf[0, at, :].astype(F32)
        sx[0, at, :] = state
        for i in range(1, NX):
            state = dxbuf[i, g:g + 1, :] * state + ubuf[i, at, :].astype(F32)
            sx[i, at, :] = state
        for n in range(HD // owned):
            piece = state[n * owned:(n + 1) * owned, :].astype(BF16)
            tslab[g * (HD // owned) + n] = piece
    tot = to_group(lambda j: tslab.at[j], tbuf, t_s, t_r)
    tbuf[zh, y] = tslab[y]
    take(late)
    project_qkc()
    attend(0)
    take(pd)
    take(tot)
    own_block = pl.ds(lax.div(y, HD // owned), 1)
    before = jnp.zeros((owned, WIDE), F32)
    for i in range(NY):
        before = pdbuf[0, i, own_block, :] * before + tbuf[0, i].astype(F32)
    carry = before * zh.astype(F32)
    for i in range(NY):
        cslab[i] = carry.astype(BF16)
        carry = pdbuf[zh, i, own_block, :] * carry + tbuf[zh, i].astype(F32)
    back = []
    for k in range(1, NY):
        j = lax.rem(y + k, NY)
        back.append(
            send(cslab.at[j], cbuf.at[y], c_s.at[k - 1], c_r.at[k - 1], tm_at(zh, j, x), head)
        )
    cbuf[y] = cslab[y]
    attend(1)
    take(back)
    for g in range(blocks):
        at = slice(g * HD, (g + 1) * HD)
        per_block = HD // owned
        came = cbuf[g * per_block:(g + 1) * per_block].reshape(HD, WIDE).astype(F32)
        for i in range(NX):
            came = dxbuf[i, g:g + 1, :] * came
            stslab[i, at, :] = (sx[i, at, :] + came).astype(BF16)
    states = []
    for k in (2, 1, 3):
        j = lax.rem(x + k, NX)
        states.append(
            send(stslab.at[j], sbuf.at[x], st_s.at[k - 1], st_r.at[k - 1], tm_at(zh, y, j), head)
        )
    sbuf[x] = stslab[x]

    def divide(i, _):
        rows = pl.ds(pl.multiple_of(i * ROWS, ROWS), ROWS)
        first, second = res[0, rows, :], res[1, rows, :]
        total = pltpu.roll(jnp.where(low, second, first), HD, 1)
        res[0, rows, :] = jnp.where(low, first, second) / total
        return 0

    lax.fori_loop(0, TOKS // ROWS, divide, 0)
    take(states)
    for g in range(NB):
        state = sbuf[g // blocks, (g % blocks) * HD:(g % blocks + 1) * HD, :].astype(F32)
        sbd[g * WIDE:g * WIDE + HD, :] = jnp.where(low, state, 0.0).astype(BF16)
        sbd[g * WIDE + HD:(g + 1) * WIDE, :] = jnp.where(low, 0.0, state).astype(BF16)
    sent = []
    for n, zz in enumerate((nearest[2], nearest[3], nearest[1], nearest[0])):
        rows = pl.ds(pl.multiple_of(zz * ROWS, ROWS), ROWS)
        ids = bidb[rows, :]
        c32 = cc[rows, :].astype(F32)
        spread = jnp.concatenate(
            [jnp.where(ids == float(g), c32, 0.0).astype(BF16) for g in range(NB)], axis=1
        )
        readout = jnp.dot(spread, sbd[...], preferred_element_type=F32) * (1.0 / 512.0)
        mixed = (res[0, rows, :] + readout).astype(BF16).reshape(CORES, LOCAL, WIDE)
        mslab[pl.ds(zz * CORES, CORES)] = mixed
        for to in (core, 1 - core):
            if n == LINE - 1 and to is core:
                continue
            dest = zz * CORES + to
            k = 2 * n + (0 if to is core else 1)
            sent.append(
                send(mslab.at[dest], mbuf.at[head], m_s.at[k], m_r.at[k], tm, dest)
            )
    mbuf[head] = mslab[head]
    wo_copy.wait()
    for move in started:
        if move not in sent:
            move.wait_send()
    take(sent)
    full = jnp.concatenate([mbuf[i] for i in range(HEADS_AXIS)], axis=1)
    out_ref[0] = jnp.dot(full, wo[...], preferred_element_type=F32).astype(BF16)

    for move in sent:
        move.wait_send()


def body(frames_in, in_weight, out_weight, block_ids, block_lists, decays):
    vmem = pl.BlockSpec(memory_space=pltpu.VMEM)
    dma = pltpu.SemaphoreType.DMA
    scratch = [
        pltpu.VMEM((1, LOCAL, D), BF16),
        pltpu.VMEM((16, 5 * WIDE), BF16),
        pltpu.VMEM((HEADS_AXIS, LOCAL, D), BF16),
        pltpu.VMEM((NZ, NY, NX, 16, 2 * WIDE), BF16),
        pltpu.VMEM((NZ, NY, NX, 16, 3 * WIDE), BF16),
        pltpu.VMEM((D, D), BF16),
        pltpu.VMEM((TOKS, WIDE), F32),
        pltpu.VMEM((WIDE, WIDE), BF16),
        pltpu.VMEM((2, TOKS, WIDE), BF16),
        pltpu.VMEM((2, TOKS, WIDE), BF16),
        pltpu.VMEM((2, TOKS, WIDE), BF16),
        pltpu.VMEM((TOKS, WIDE), BF16),
        pltpu.VMEM((WIDE, NB * WIDE), F32),
        pltpu.VMEM((2, TOKS, WIDE), F32),
        pltpu.VMEM((NX, 256, WIDE), BF16),
        pltpu.VMEM((NX, 256, WIDE), BF16),
        pltpu.VMEM((NX, 256, WIDE), F32),
        pltpu.VMEM((NY, 32, WIDE), BF16),
        pltpu.VMEM((NZ, NY, 32, WIDE), BF16),
        pltpu.VMEM((NY, 32, WIDE), BF16),
        pltpu.VMEM((NY, 32, WIDE), BF16),
        pltpu.VMEM((NX, 256, WIDE), BF16),
        pltpu.VMEM((NX, 256, WIDE), BF16),
        pltpu.VMEM((NB * WIDE, WIDE), BF16),
        pltpu.VMEM((HEADS_AXIS, LOCAL, WIDE), BF16),
        pltpu.VMEM((HEADS_AXIS, LOCAL, WIDE), BF16),
        pltpu.VMEM((NX, 8, WIDE), F32),
        pltpu.VMEM((NX, 8, WIDE), F32),
        pltpu.VMEM((8, WIDE), F32),
        pltpu.VMEM((NZ, NY, 8, WIDE), F32),
    ]
    for shape in (
        (2,), (2, 2, NX - 1), (2, 2, NY - 1), (2, LINE - 1, CHUNKS),
        (2 * LINE - 1, PAIRS),
        (NX - 1,), (2, NY), (NX - 1,), (2, NY), (NY - 1,), (NX - 1,), (HEADS_AXIS,),
    ):
        scratch += [dma(shape), dma(shape)]
    scratch.append(dma((3,)))
    hbm = pl.BlockSpec(memory_space=pl.ANY)
    return pl.pallas_call(
        kernel,
        out_shape=jax.ShapeDtypeStruct((1, LOCAL, D), BF16),
        in_specs=[hbm, hbm, hbm, vmem, vmem, vmem],
        out_specs=vmem,
        scratch_shapes=scratch,
        compiler_params=pltpu.CompilerParams(
            collective_id=0, has_side_effects=True, vmem_limit_bytes=56 * 1024 * 1024
        ),
        name="layer",
    )(frames_in, in_weight, out_weight, block_ids.reshape(1, TOKS), block_lists.T, decays)


def solution(mesh):
    return jax.shard_map(
        body,
        mesh=mesh,
        in_specs=(P("tm", "head", None), P("tm", "head"), P(), P(), P(), P("tm", "head", None)),
        out_specs=P("tm", "head", None),
        check_vma=False,
    )
```

```python
import functools

import jax
import jax.numpy as jnp
from jax import lax
from jax.experimental import pallas as pl
from jax.experimental.pallas import tpu as pltpu
from jax.sharding import PartitionSpec as P

HD = 64
NB = 16
D = 1024
TOKS = 1024
LOCAL = 128
WIDE = 2 * HD
NX, NY, NZ = 4, 8, 2
NG = NY * NZ
LINE, CORES = 4, 2
HEADS_AXIS = LINE * CORES
CHUNKS = 4
PAIRS = 2
ROWS = 256
EPS = 1e-6
FAR = -256.0
F32, BF16 = jnp.float32, jnp.bfloat16
MESH = pl.DeviceIdType.MESH


class Move:
    def __init__(self, copy, go=None, come=None):
        self.copy, self.go, self.come, self.took = copy, go, come, False

    def start(self):
        self.copy.start() if self.go is None else pl.when(self.go)(self.copy.start)

    def wait_recv(self):
        self.took = True
        self.copy.wait_recv() if self.come is None else pl.when(self.come)(self.copy.wait_recv)

    def wait_send(self):
        self.copy.wait_send() if self.go is None else pl.when(self.go)(self.copy.wait_send)


def kernel(
    x_hbm, w_hbm, wo_hbm, bid_ref, lists_ref, dec_ref, out_ref,
    xin, win, xbuf, wvb, wqkc, wo, bidb, fmat, qa, ka, va, cc, acc, res,
    sslab, ubuf, sx, tslab, tbuf, cslab, cbuf, stslab, sbuf, sbd, mslab, mbuf,
    dout, dxbuf, pdout, pdbuf,
    wz_s, wz_r, wx_s, wx_r, wy_s, wy_r, xg_s, xg_r, sib_s, sib_r,
    dx_s, dx_r, pd_s, pd_r, u_s, u_r, t_s, t_r, c_s, c_r, st_s, st_r, m_s, m_r, in_sem,
):
    tm, head = lax.axis_index("tm"), lax.axis_index("head")
    x, r = lax.rem(tm, NX), lax.div(tm, NX)
    y, zh = lax.rem(r, NY), lax.div(r, NY)
    z, core = lax.div(head, CORES), lax.rem(head, CORES)

    def tm_at(zz, yy, xx):
        return (zz * NY + yy) * NX + xx

    barrier = pltpu.get_barrier_semaphore()

    def greet(tm_to, head_to):
        pl.semaphore_signal(barrier, inc=1, device_id=(tm_to, head_to), device_id_type=MESH)

    first_half, second_half = zh == 0, zh == 1
    pl.when(first_half)(lambda: greet(tm_at(1 - zh, y, x), head))
    greet(tm_at(zh, y, lax.rem(x + 2, NX)), head)
    for k in (1, NX - 1):
        greet(tm_at(zh, y, lax.rem(x + k, NX)), head)
    for k in (4, 3, 5, 2, 6, 1, 7):
        greet(tm_at(zh, lax.rem(y + k, NY), x), head)
    pl.when(z > 0)(lambda: greet(tm, head - CORES))
    pl.when(z < LINE - 1)(lambda: greet(tm, head + CORES))
    greet(tm, z * CORES + 1 - core)
    expected = 11 + zh + (z > 0).astype(jnp.int32) + (z < LINE - 1).astype(jnp.int32)

    loads = [
        pltpu.make_async_copy(src, dst, in_sem.at[i])
        for i, (src, dst) in enumerate(((w_hbm, win), (x_hbm, xin), (wo_hbm, wo)))
    ]
    for load in loads:
        load.start()
    wo_copy = loads[2]
    started = []

    def send(src, dst, ssem, rsem, tm_to, head_to, go=None, come=None):
        move = Move(
            pltpu.make_async_remote_copy(
                src_ref=src, dst_ref=dst, send_sem=ssem, recv_sem=rsem,
                device_id=(tm_to, head_to), device_id_type=MESH,
            ), go, come,
        )
        move.start()
        started.append(move)
        return move

    lane = lax.broadcasted_iota(jnp.int32, (1, WIDE), 1)
    low = lane < HD

    loads[0].wait()
    raw = [win[:, i * WIDE:(i + 1) * WIDE].astype(F32) for i in range(5)]
    swap = functools.partial(pltpu.roll, shift=HD, axis=1)
    ordered = [
        jnp.where(low, raw[1], raw[3]),
        swap(jnp.where(low, raw[4], raw[1])),
        jnp.where(low, raw[0], raw[2]),
        swap(jnp.where(low, raw[3], raw[0])),
        jnp.where(low, raw[2], raw[4]),
    ]
    for i in range(5):
        buf, col = (wvb, i) if i < 2 else (wqkc, i - 2)
        buf[zh, y, x, :, col * WIDE:(col + 1) * WIDE] = ordered[i].astype(BF16)


    def part(source, k, size=LOCAL // CHUNKS):
        return xbuf.at[source * CORES + core, pl.ds(k * size, size)]

    def is_source(zz):
        return (zz >= 0) & (zz < LINE)

    line, sib = {}, {}

    def send_line(way, s, k):
        source, to = (z - (s - 1), z + 1) if way == 0 else (z + (s - 1), z - 1)
        come = is_source(z - s if way == 0 else z + s)
        ref = part(source, k)
        line[way, s, k] = send(
            ref, ref, xg_s.at[way, s - 1, k], xg_r.at[way, s - 1, k], tm, to * CORES + core,
            is_source(source) & is_source(to), come,
        )

    def send_sib(n, source, k, go=None, come=None):
        ref = part(source, k, LOCAL // PAIRS)
        sib[n, k] = send(
            ref, ref, sib_s.at[n, k], sib_r.at[n, k], tm, z * CORES + 1 - core, go, come
        )

    def take_line(s, k):
        for way in range(2):
            move = line[way, s, k]
            move.wait_recv()
            if s < LINE - 1:
                send_line(way, s + 1, k)
            if k % (CHUNKS // PAIRS) == CHUNKS // PAIRS - 1:
                send_sib(
                    2 * s - 1 + way, z - s if way == 0 else z + s, k // (CHUNKS // PAIRS),
                    move.come, move.come,
                )

    parts = (wvb, wqkc)

    def send_z(c, go, come):
        ref = parts[c].at[zh, y, x]
        return [send(ref, ref, wz_s.at[c], wz_r.at[c], tm_at(1 - zh, y, x), head, go, come)]

    def send_piece(c, side):
        ref = parts[c].at[zh if side == 0 else 1 - zh, y, x]
        return [
            send(ref, ref, wy_s.at[c, side, k - 1], wy_r.at[c, side, k - 1],
                 tm_at(zh, lax.rem(y + k, NY), x), head)
            for k in (4, 3, 5, 2, 6, 1, 7)
        ]

    def take(moves):
        for move in moves:
            move.wait_recv()

    def send_bulk(c, side):
        ref = parts[c].at[zh if side == 0 else 1 - zh, :, x]
        return [
            send(ref, ref, wx_s.at[c, side, k - 1], wx_r.at[c, side, k - 1],
                 tm_at(zh, y, lax.rem(x + k, NX)), head)
            for k in (2, 1, 3)
        ]

    pl.semaphore_wait(barrier, expected)
    far = send_z(0, second_half, first_half)
    own = send_piece(0, 0)
    loads[1].wait()
    wide = xin[0].astype(F32)
    xbuf[head] = (
        wide * lax.rsqrt(jnp.mean(wide * wide, axis=-1, keepdims=True) + EPS)
    ).astype(BF16)
    for k in range(CHUNKS):
        for way in range(2):
            send_line(way, 1, k)
    for k in range(PAIRS):
        send_sib(0, z, k)
    far_late = send_z(1, second_half, first_half)
    own_late = send_piece(1, 0)
    take(own)
    direct = send_bulk(0, 0)

    dec = dec_ref[0]
    gi = lax.broadcasted_iota(jnp.int32, (NB, NB), 0)
    gj = lax.broadcasted_iota(jnp.int32, (NB, NB), 1)
    cols = [
        jnp.sum(jnp.where(gi == gj, dec[h:h + 1, :], 0.0), axis=1, keepdims=True) for h in range(2)
    ]
    drow = jnp.where(low, cols[0], cols[1])
    dout[...] = jnp.zeros_like(dout)
    for j in range(NX):
        dout[j, 0:4, :] = drow[4 * j:4 * j + 4, :]
    dxbuf[x] = dout[x]

    dx = []
    for k in range(1, NX):
        j = lax.rem(x + k, NX)
        dx.append(
            send(dout.at[j], dxbuf.at[x], dx_s.at[k - 1], dx_r.at[k - 1], tm_at(zh, y, j), head)
        )
    take_line(1, 0)
    take_line(1, 1)

    ids = jnp.broadcast_to(bid_ref[...].astype(F32), (WIDE, TOKS))
    for i in range(TOKS // WIDE):
        bidb[i * WIDE:(i + 1) * WIDE, :] = ids[:, i * WIDE:(i + 1) * WIDE].T
    fmat[...] = jnp.zeros_like(fmat)
    wrapped = lane & (HD - 1)
    wrapped_f = wrapped.astype(F32)
    key_block = lax.broadcasted_iota(jnp.int32, (WIDE, NB), 0) & (HD - 1)
    adjacent = key_block >= NB
    for k in range(lists_ref.shape[0]):
        adjacent = adjacent | (lists_ref[k:k + 1, :] == key_block)
    fmat[:, 0:NB] = jnp.where(adjacent, 0.0, FAR).astype(BF16)

    take_line(1, 2)
    take(own_late)
    late = send_bulk(1, 0)
    take_line(1, 3)
    take(dx)
    prod = dxbuf[0]
    for i in range(1, NX):
        prod = prod * dxbuf[i]
    pdout[...] = prod
    pdbuf[zh, y] = prod
    for k in range(CHUNKS):
        take_line(2, k)
    take(far)
    take(send_z(0, first_half, second_half))
    other = send_piece(0, 1)
    take(far_late)
    far_late = send_z(1, first_half, second_half)
    take_line(3, 0)
    take(other)
    direct += send_bulk(0, 1)
    take(far_late)
    other_late = send_piece(1, 1)
    take_line(3, 1)
    take(direct)
    take(other_late)
    late += send_bulk(1, 1)

    def to_group(src_of, dst, ssem, rsem):
        moves = []
        for k in range(NY):
            j = lax.rem(y + k, NY)
            moves.append(
                send(src_of(j), dst.at[0, y], ssem.at[1, k], rsem.at[1, k], tm_at(1, j, x), head,
                     first_half, second_half)
            )
        for k in range(1, NY):
            j = lax.rem(y + k, NY)
            moves.append(
                send(src_of(j), dst.at[zh, y], ssem.at[0, k], rsem.at[0, k], tm_at(zh, j, x), head)
            )
        return moves

    def project_vb(zz, first):
        rows = pl.ds(pl.multiple_of(zz * ROWS, ROWS), ROWS)
        tokens = xbuf[pl.ds(zz * CORES, CORES)].reshape(ROWS, D)
        weights = wvb[...].reshape(D, 2 * WIDE)
        p = jnp.dot(tokens, weights, preferred_element_type=F32).astype(BF16).astype(F32)
        v, b = p[:, 0:WIDE], p[:, WIDE:2 * WIDE]
        ids = bidb[rows, :]
        va[0, rows, :] = jnp.where(low, v, 1.0).astype(BF16)
        va[1, rows, :] = jnp.where(low, 1.0, v).astype(BF16)
        bt = b.T.astype(BF16)
        for g in range(0, NB, 4):
            masked = jnp.concatenate(
                [jnp.where(ids == float(g + n), v, 0.0).astype(BF16) for n in range(4)], axis=1
            )
            at = slice(g * WIDE, (g + 4) * WIDE)
            term = jnp.dot(bt, masked, preferred_element_type=F32)
            acc[:, at] = term if first else acc[:, at] + term

    odd = lax.rem(z, 2)
    nearest = (z, z + 1 - 2 * odd, lax.rem(z + 2, LINE), 3 - z)
    for n in range(LINE):
        if 0 < n < LINE - 1:
            take_line(3, n + 1)
        for way in range(2) if n else (0,):
            for k in range(PAIRS):
                sib[2 * n - 1 + way if n else 0, k].wait_recv()
        project_vb(nearest[n], n == 0)

    for g in range(NB):
        at = slice(g * WIDE, (g + 1) * WIDE)
        both = jnp.where(low, acc[0:HD, at], acc[HD:WIDE, at])
        sslab[g // 4, (g % 4) * HD:(g % 4 + 1) * HD, :] = both.astype(BF16)
    up = []
    for k in (2, 1, 3):
        j = lax.rem(x + k, NX)
        up.append(
            send(sslab.at[j], ubuf.at[x], u_s.at[k - 1], u_r.at[k - 1], tm_at(zh, y, j), head)
        )
    ubuf[x] = sslab[x]
    pd = to_group(lambda j: pdout, pdbuf, pd_s, pd_r)

    def normed_heads(values):
        square = values * values
        means = [
            jnp.sum(jnp.where(keep, square, 0.0), axis=-1, keepdims=True) * (1.0 / HD)
            for keep in (low, ~low)
        ]
        return (values * lax.rsqrt(jnp.where(low, means[0], means[1]) + EPS)).astype(BF16).astype(F32)

    def project_qkc():
        tokens = xbuf[...].reshape(TOKS, D)
        weights = wqkc[...].reshape(D, 3 * WIDE)
        p = jnp.dot(tokens, weights, preferred_element_type=F32).astype(BF16)
        q, k, c = (p[:, j * WIDE:(j + 1) * WIDE] for j in range(3))
        hot = jnp.where(bidb[...] == wrapped_f, 1.0, 0.0)
        banned = lax.dot_general(
            hot.astype(BF16), fmat[...], (((1,), (1,)), ((), ())), preferred_element_type=F32
        )
        qn = normed_heads(q.astype(F32)) * 0.125
        kn = normed_heads(k.astype(F32))
        qa[0, :, :] = jnp.where(low, qn, banned).astype(BF16)
        qa[1, :, :] = jnp.where(low, banned, qn).astype(BF16)
        ka[0, :, :] = jnp.where(low, kn, hot).astype(BF16)
        ka[1, :, :] = jnp.where(low, hot, kn).astype(BF16)
        cc[...] = c

    def attend(h):
        score = lax.dot_general(
            qa[h], ka[h], (((1,), (1,)), ((), ())), preferred_element_type=F32
        )
        res[h] = jnp.dot(jnp.exp(score).astype(BF16), va[h], preferred_element_type=F32)

    take(up)
    blocks, owned = NB // NX, 32
    for g in range(blocks):
        at = slice(g * HD, (g + 1) * HD)
        state = ubuf[0, at, :].astype(F32)
        sx[0, at, :] = state
        for i in range(1, NX):
            state = dxbuf[i, g:g + 1, :] * state + ubuf[i, at, :].astype(F32)
            sx[i, at, :] = state
        for n in range(HD // owned):
            piece = state[n * owned:(n + 1) * owned, :].astype(BF16)
            tslab[g * (HD // owned) + n] = piece
    tot = to_group(lambda j: tslab.at[j], tbuf, t_s, t_r)
    tbuf[zh, y] = tslab[y]
    take(late)
    project_qkc()
    take(pd)
    take(tot)
    own_block = pl.ds(lax.div(y, HD // owned), 1)
    before = jnp.zeros((owned, WIDE), F32)
    for i in range(NY):
        before = pdbuf[0, i, own_block, :] * before + tbuf[0, i].astype(F32)
    carry = before * zh.astype(F32)
    for i in range(NY):
        cslab[i] = carry.astype(BF16)
        carry = pdbuf[zh, i, own_block, :] * carry + tbuf[zh, i].astype(F32)
    back = []
    for k in range(1, NY):
        j = lax.rem(y + k, NY)
        back.append(
            send(cslab.at[j], cbuf.at[y], c_s.at[k - 1], c_r.at[k - 1], tm_at(zh, j, x), head)
        )
    cbuf[y] = cslab[y]
    attend(0)
    attend(1)
    take(back)
    for g in range(blocks):
        at = slice(g * HD, (g + 1) * HD)
        per_block = HD // owned
        came = cbuf[g * per_block:(g + 1) * per_block].reshape(HD, WIDE).astype(F32)
        for i in range(NX):
            came = dxbuf[i, g:g + 1, :] * came
            stslab[i, at, :] = (sx[i, at, :] + came).astype(BF16)
    states = []
    for k in (2, 1, 3):
        j = lax.rem(x + k, NX)
        states.append(
            send(stslab.at[j], sbuf.at[x], st_s.at[k - 1], st_r.at[k - 1], tm_at(zh, y, j), head)
        )
    sbuf[x] = stslab[x]

    def divide(i, _):
        rows = pl.ds(pl.multiple_of(i * ROWS, ROWS), ROWS)
        first, second = res[0, rows, :], res[1, rows, :]
        total = pltpu.roll(jnp.where(low, second, first), HD, 1)
        res[0, rows, :] = jnp.where(low, first, second) / total
        return 0

    lax.fori_loop(0, TOKS // ROWS, divide, 0)
    take(states)
    for g in range(NB):
        state = sbuf[g // blocks, (g % blocks) * HD:(g % blocks + 1) * HD, :].astype(F32)
        sbd[g * WIDE:g * WIDE + HD, :] = jnp.where(low, state, 0.0).astype(BF16)
        sbd[g * WIDE + HD:(g + 1) * WIDE, :] = jnp.where(low, 0.0, state).astype(BF16)
    sent = []
    for n, zz in enumerate((nearest[2], nearest[3], nearest[1], nearest[0])):
        rows = pl.ds(pl.multiple_of(zz * ROWS, ROWS), ROWS)
        ids = bidb[rows, :]
        c32 = cc[rows, :].astype(F32)
        spread = jnp.concatenate(
            [jnp.where(ids == float(g), c32, 0.0).astype(BF16) for g in range(NB)], axis=1
        )
        readout = jnp.dot(spread, sbd[...], preferred_element_type=F32) * (1.0 / 512.0)
        mixed = (res[0, rows, :] + readout).astype(BF16).reshape(CORES, LOCAL, WIDE)
        mslab[pl.ds(zz * CORES, CORES)] = mixed
        for to in (core, 1 - core):
            if n == LINE - 1 and to is core:
                continue
            dest = zz * CORES + to
            k = 2 * n + (0 if to is core else 1)
            sent.append(
                send(mslab.at[dest], mbuf.at[head], m_s.at[k], m_r.at[k], tm, dest)
            )
    mbuf[head] = mslab[head]
    wo_copy.wait()
    for move in started:
        if move not in sent:
            move.wait_send()
    take(sent)
    full = jnp.concatenate([mbuf[i] for i in range(HEADS_AXIS)], axis=1)
    out_ref[0] = jnp.dot(full, wo[...], preferred_element_type=F32).astype(BF16)

    for move in sent:
        move.wait_send()


def body(frames_in, in_weight, out_weight, block_ids, block_lists, decays):
    vmem = pl.BlockSpec(memory_space=pltpu.VMEM)
    dma = pltpu.SemaphoreType.DMA
    scratch = [
        pltpu.VMEM((1, LOCAL, D), BF16),
        pltpu.VMEM((16, 5 * WIDE), BF16),
        pltpu.VMEM((HEADS_AXIS, LOCAL, D), BF16),
        pltpu.VMEM((NZ, NY, NX, 16, 2 * WIDE), BF16),
        pltpu.VMEM((NZ, NY, NX, 16, 3 * WIDE), BF16),
        pltpu.VMEM((D, D), BF16),
        pltpu.VMEM((TOKS, WIDE), F32),
        pltpu.VMEM((WIDE, WIDE), BF16),
        pltpu.VMEM((2, TOKS, WIDE), BF16),
        pltpu.VMEM((2, TOKS, WIDE), BF16),
        pltpu.VMEM((2, TOKS, WIDE), BF16),
        pltpu.VMEM((TOKS, WIDE), BF16),
        pltpu.VMEM((WIDE, NB * WIDE), F32),
        pltpu.VMEM((2, TOKS, WIDE), F32),
        pltpu.VMEM((NX, 256, WIDE), BF16),
        pltpu.VMEM((NX, 256, WIDE), BF16),
        pltpu.VMEM((NX, 256, WIDE), F32),
        pltpu.VMEM((NY, 32, WIDE), BF16),
        pltpu.VMEM((NZ, NY, 32, WIDE), BF16),
        pltpu.VMEM((NY, 32, WIDE), BF16),
        pltpu.VMEM((NY, 32, WIDE), BF16),
        pltpu.VMEM((NX, 256, WIDE), BF16),
        pltpu.VMEM((NX, 256, WIDE), BF16),
        pltpu.VMEM((NB * WIDE, WIDE), BF16),
        pltpu.VMEM((HEADS_AXIS, LOCAL, WIDE), BF16),
        pltpu.VMEM((HEADS_AXIS, LOCAL, WIDE), BF16),
        pltpu.VMEM((NX, 8, WIDE), F32),
        pltpu.VMEM((NX, 8, WIDE), F32),
        pltpu.VMEM((8, WIDE), F32),
        pltpu.VMEM((NZ, NY, 8, WIDE), F32),
    ]
    for shape in (
        (2,), (2, 2, NX - 1), (2, 2, NY - 1), (2, LINE - 1, CHUNKS),
        (2 * LINE - 1, PAIRS),
        (NX - 1,), (2, NY), (NX - 1,), (2, NY), (NY - 1,), (NX - 1,), (HEADS_AXIS,),
    ):
        scratch += [dma(shape), dma(shape)]
    scratch.append(dma((3,)))
    hbm = pl.BlockSpec(memory_space=pl.ANY)
    return pl.pallas_call(
        kernel,
        out_shape=jax.ShapeDtypeStruct((1, LOCAL, D), BF16),
        in_specs=[hbm, hbm, hbm, vmem, vmem, vmem],
        out_specs=vmem,
        scratch_shapes=scratch,
        compiler_params=pltpu.CompilerParams(
            collective_id=0, has_side_effects=True, vmem_limit_bytes=56 * 1024 * 1024
        ),
        name="layer",
    )(frames_in, in_weight, out_weight, block_ids.reshape(1, TOKS), block_lists.T, decays)


def solution(mesh):
    return jax.shard_map(
        body,
        mesh=mesh,
        in_specs=(P("tm", "head", None), P("tm", "head"), P(), P(), P(), P("tm", "head", None)),
        out_specs=P("tm", "head", None),
        check_vma=False,
    )
```
